32 devices in a mesh: req: 8 (over z, y), head: 4 (over x, core).
Axes of the slice: x: 2, y: 2, z: 4, core: 2. Of those that a mesh axis runs over, the one named last changes fastest.
Arguments:
- hidden: bfloat16 [1024, 6144], P('req'), may hold values from -15 to 15
- attn_norm_gain: float32 [6144], replicated, may hold values from 0.3 to 3
- attn_norm_bias: float32 [6144], replicated, may hold values from -4 to 4
- mlp_norm_gain: float32 [6144], replicated, may hold values from 0.3 to 3
- mlp_norm_bias: float32 [6144], replicated, may hold values from -4 to 4
- qkv_weight: bfloat16 [6144, 9216], P('req', 'head'), may hold values from -0.078125 to 0.078125
- qkv_bias: float32 [9216], P('head'), may hold values from -3 to 3
- out_weight: bfloat16 [3072, 6144], P('head', 'req'), may hold values from -0.625 to 0.625
- out_bias: float32 [6144], replicated, may hold values from -3 to 3
- up_weight: bfloat16 [6144, 12288], P('req', 'head'), may hold values from -0.078125 to 0.078125
- up_bias: float32 [12288], P('head'), may hold values from -3 to 3
- down_weight: bfloat16 [12288, 6144], P('head', 'req'), may hold values from -0.0546875 to 0.0546875
- down_bias: float32 [6144], replicated, may hold values from -3 to 3
- cache_keys: bfloat16 [8, 4096, 3072], P('req', None, 'head'), may hold values from -1300 to 1300
- cache_values: bfloat16 [8, 4096, 3072], P('req', None, 'head'), may hold values from -6 to 6
- cached_len: int32 [8], P('req'), may hold values from 128 to 4096, as said below
Outputs:
- hidden_out: bfloat16 [1024, 6144], P('req')
- new_keys: bfloat16 [8, 128, 3072], P('req', None, 'head')
- new_values: bfloat16 [8, 128, 3072], P('req', None, 'head')
The draws below stay inside these ranges and needn't reach their ends.
Inputs may be any that keep to these rules, and one draw needn't show every extreme that they name: `cached_len`: each entry is 128 or 4096, and both values occur.
All inputs are finite; a program needn't handle non-finite values.
Results may differ from the reference program's by a relative error of at most 0.0085.
The reference program's roundings to bfloat16 on the way count: a program that leaves them out, or rounds other values in their place, can miss the bound.
Values may be sent and summed in bfloat16 or wider, within the bound.
No kernel may reach another device: no remote copies, remote signals or barrier semaphores. Data moves between devices by JAX's collectives and lax.ppermute only.
A program may use at most 128 MiB of HBM per device.

```python
import math
import jax
import jax.numpy as jnp
from jax import lax

D = 6144
HEADS = 32
DH = 96
ROT = 24
FF = 12288
NEW = 128
CACHE = 4096
SHORT = 128
REQS = 8
TOKENS = 1024


def draw_hidden(key, part):
    base_key = jax.random.fold_in(key, 11)
    key_main, key_rows, key_cols = jax.random.split(base_key, 3)
    rows_scale = 0.1 * jnp.exp(jax.random.uniform(key_rows, (TOKENS, 1), jnp.float32) * jnp.log(10.0))
    cols_scale = 0.3 * jnp.exp(jax.random.uniform(key_cols, (1, D), jnp.float32) * jnp.log(10.0))
    base_values = jax.random.normal(key_main, (TOKENS, D), jnp.float32)
    return (jnp.clip(base_values, -5.0, 5.0) * rows_scale * cols_scale).astype(jnp.bfloat16)


def draw_cache_keys(key, part):
    base_key = jax.random.fold_in(key, 23)
    key_main = jax.random.fold_in(base_key, 0)
    base_values = jnp.clip(jax.random.normal(key_main, (REQS, CACHE, HEADS * DH), jnp.float32), -6.0, 6.0)
    return base_values.astype(jnp.bfloat16)


def draw_cached_len(key, part):
    base_key = jax.random.fold_in(key, 37)
    key_long, key_pick = jax.random.split(base_key, 2)
    request_index = jnp.arange(REQS, dtype=jnp.int32)
    chosen = jax.random.randint(key_pick, (), 0, REQS, dtype=jnp.int32)
    long_ones = jax.random.randint(key_long, (REQS,), 0, 4, dtype=jnp.int32) == 0
    long_ones = jnp.logical_or(long_ones, request_index == chosen)
    long_ones = jnp.logical_and(long_ones, request_index != (chosen + 1) % REQS)
    return jnp.where(long_ones, CACHE, SHORT).astype(jnp.int32)


def block_levels(key, extent, cuts, low, largest):
    level = 1.0
    for axis_at, parts in cuts:
        heights = jax.random.uniform(jax.random.fold_in(jax.random.fold_in(key, 6), axis_at), (parts,), jnp.float32, low / len(cuts), largest / len(cuts))
        level = level * jnp.repeat(jnp.exp(heights), extent[axis_at] // parts).reshape((-1,) + (1,) * (len(extent) - 1 - axis_at))
    return level


def noise(rng, extent, scale, most, pieces=(), kind=jnp.bfloat16):
    drawn = jax.random.normal(rng, extent, jnp.float32) * scale
    if len(pieces) > 0:
        drawn = block_levels(rng, extent, pieces, -0.22, 0.18) * drawn
    return jnp.clip(drawn, min=-most, max=most).astype(kind)


def setup_inputs(seed: int = 0) -> dict:
    splits = jax.random.split(jax.random.key(seed), 17)
    hidden = draw_hidden(jax.random.fold_in(splits[16], 71), 0)
    attn_norm_gain = jnp.clip(jnp.exp(jax.random.uniform(splits[1], (D,), jnp.float32, math.log(0.3), math.log(3.0))), 0.3, 3.0)
    attn_norm_bias = noise(splits[2], (D,), 1.0, 4.0, (), jnp.float32)
    mlp_norm_gain = jnp.clip(jnp.exp(jax.random.uniform(splits[3], (D,), jnp.float32, math.log(0.3), math.log(3.0))), 0.3, 3.0)
    mlp_norm_bias = noise(splits[4], (D,), 1.0, 4.0, (), jnp.float32)
    qkv_weight = noise(splits[5], (D, HEADS * 3 * DH), D ** -0.5, 0.078125, ((0, 8), (1, 4)))
    qkv_bias = noise(splits[6], (HEADS * 3 * DH,), 0.5, 3.0, ((0, 4),), jnp.float32)
    out_weight = noise(splits[7], (HEADS * DH, D), DH ** -0.5, 0.625, ((0, 4), (1, 8)))
    out_bias = noise(splits[8], (D,), 0.5, 3.0, (), jnp.float32)
    up_weight = noise(splits[9], (D, FF), D ** -0.5, 0.078125, ((0, 8), (1, 4)))
    up_bias = noise(splits[10], (FF,), 0.5, 3.0, ((0, 4),), jnp.float32)
    down_weight = noise(splits[11], (FF, D), FF ** -0.5, 0.0546875, ((0, 4), (1, 8)))
    down_bias = noise(splits[12], (D,), 0.5, 3.0, (), jnp.float32)
    cache_keys = draw_cache_keys(jax.random.fold_in(splits[16], 71), 0)
    cache_values = noise(splits[14], (REQS, CACHE, HEADS * DH), 1.0, 6.0, ((0, 8), (2, 4)))
    cached_len = draw_cached_len(jax.random.fold_in(splits[16], 71), 0)
    return dict(hidden=hidden, attn_norm_gain=attn_norm_gain, attn_norm_bias=attn_norm_bias, mlp_norm_gain=mlp_norm_gain, mlp_norm_bias=mlp_norm_bias, qkv_weight=qkv_weight, qkv_bias=qkv_bias, out_weight=out_weight, out_bias=out_bias, up_weight=up_weight, up_bias=up_bias, down_weight=down_weight, down_bias=down_bias, cache_keys=cache_keys, cache_values=cache_values, cached_len=cached_len)


def normalize(values, norm_gain, norm_shift):
    widened = values.astype(jnp.float32)
    center = lax.optimization_barrier(jnp.mean(widened, axis=-1, keepdims=True))
    spread = lax.optimization_barrier(jnp.mean(jnp.square(widened - center), axis=-1, keepdims=True))
    return ((widened - center) * lax.rsqrt(spread + 1e-05) * norm_gain + norm_shift).astype(jnp.bfloat16)

def rotate(values, position):
    halfway = ROT // 2
    exponent = jnp.arange(halfway, dtype=jnp.float32) * (2.0 / ROT)
    frequency = jnp.power(10000.0, -exponent)
    angle = position[:, None] * frequency[None, :]
    cosine = jnp.cos(angle)[:, None, :]
    sine_part = jnp.sin(angle)[:, None, :]
    lower_half = values[..., :halfway]
    upper_half = values[..., halfway:ROT]
    return jnp.concatenate([lower_half * cosine - upper_half * sine_part, upper_half * cosine + lower_half * sine_part, values[..., ROT:]], axis=-1)

def attend_one(inputs):
    qkv_rows, keys_old, values_old, length = inputs
    position = length.astype(jnp.float32) + jnp.arange(NEW, dtype=jnp.float32)
    queries = rotate(qkv_rows[:, :, 0], position).astype(jnp.bfloat16)
    key_new = rotate(qkv_rows[:, :, 1], position).astype(jnp.bfloat16)
    value_new = qkv_rows[:, :, 2].astype(jnp.bfloat16)
    all_keys = jnp.concatenate([keys_old, key_new], axis=0).astype(jnp.float32)
    all_values = jnp.concatenate([values_old, value_new], axis=0).astype(jnp.float32)
    scores = jnp.einsum('qhd,khd->hqk', queries.astype(jnp.float32), all_keys) * (1.0 / math.sqrt(DH))
    key_index = jnp.arange(CACHE + NEW, dtype=jnp.int32)
    query_index = jnp.arange(NEW, dtype=jnp.int32)
    visible = jnp.where(key_index[None, :] < CACHE, key_index[None, :] < length, key_index[None, :] - CACHE <= query_index[:, None])
    scores = jnp.where(visible[None], scores, -1e+30)
    highest = lax.optimization_barrier(jnp.max(scores, axis=-1, keepdims=True))
    weights = jnp.exp(scores - highest)
    totals = lax.optimization_barrier(jnp.sum(weights, axis=-1))
    rounded = lax.optimization_barrier(weights.astype(jnp.bfloat16)).astype(jnp.float32)
    mixed = jnp.einsum('hqk,khd->qhd', rounded, all_values) / jnp.transpose(totals)[:, :, None]
    return (mixed.astype(jnp.bfloat16).reshape(NEW, HEADS * DH), key_new.reshape(NEW, HEADS * DH), value_new.reshape(NEW, HEADS * DH))

def reference(hidden, attn_norm_gain, attn_norm_bias, mlp_norm_gain, mlp_norm_bias, qkv_weight, qkv_bias, out_weight, out_bias, up_weight, up_bias, down_weight, down_bias, cache_keys, cache_values, cached_len):
    attn_normed = normalize(hidden, attn_norm_gain, attn_norm_bias)
    mlp_normed = normalize(hidden, mlp_norm_gain, mlp_norm_bias)
    qkv = jnp.dot(attn_normed, qkv_weight, preferred_element_type=jnp.float32) + qkv_bias
    up_sum = jnp.dot(mlp_normed, up_weight, preferred_element_type=jnp.float32) + up_bias
    units = jax.nn.gelu(up_sum, approximate=True).astype(jnp.bfloat16)
    per_request = qkv.reshape(REQS, NEW, HEADS, 3, DH)
    keys_old = cache_keys.reshape(REQS, CACHE, HEADS, DH)
    values_old = cache_values.reshape(REQS, CACHE, HEADS, DH)
    attended, new_keys, new_values = lax.map(attend_one, (per_request, keys_old, values_old, cached_len))
    attended = attended.reshape(TOKENS, HEADS * DH)
    attention = jnp.dot(attended, out_weight, preferred_element_type=jnp.float32)
    feed_forward = jnp.dot(units, down_weight, preferred_element_type=jnp.float32)
    hidden_out = (hidden.astype(jnp.float32) + attention + out_bias + feed_forward + down_bias).astype(jnp.bfloat16)
    return (hidden_out, new_keys, new_values)
```

```python
import functools
import math

import jax
import jax.numpy as jnp
import numpy as np
from jax import lax
from jax.experimental import pallas as pl
from jax.experimental.pallas import tpu as pltpu
from jax.sharding import PartitionSpec as P

DH = 96
ROT = 24
NEW = 128
CACHE = 4096
SHORT = 128
GROUP = 4 * DH
LANE = 128
KEYS = 512
F32 = jnp.float32
BF16 = jnp.bfloat16


def ring_order(size):
    inner = 1
    while 4 * inner * inner <= size:
        inner *= 2
    outer = size // inner
    order = [a * inner for a in range(outer)]
    forward = True
    for a in reversed(range(outer)):
        row = list(range(1, inner))
        order += [a * inner + b for b in (row if forward else row[::-1])]
        forward = not forward
    return order


class Ring:
    def __init__(self, size):
        self.size = size
        self.order = ring_order(size)
        place = np.zeros(size, np.int32)
        place[self.order] = np.arange(size)
        self.here = jnp.asarray(place)[lax.axis_index("req")]
        self.table = jnp.asarray(np.array(self.order, np.int32))

    def block(self, distance):
        return self.table[(self.here + distance) % self.size]

    def shift(self, values, distance):
        n = self.size
        pairs = [(self.order[i], self.order[(i + distance) % n]) for i in range(n)]
        return lax.ppermute(values, "req", pairs)


class Cube:
    def __init__(self, size):
        self.size = size
        self.bits = size.bit_length() - 1
        self.index = lax.axis_index("head")

    def swap(self, values, bit):
        return lax.ppermute(values, "head", [(i, i ^ (1 << bit)) for i in range(self.size)])

    def gather(self, values):
        count, rows, width = values.shape
        gathered = values
        for done, bit in enumerate(reversed(range(self.bits))):
            other = self.swap(gathered, bit)
            upper = ((self.index >> bit) & 1) == 1
            gathered = jnp.stack(
                [jnp.where(upper, other, gathered), jnp.where(upper, gathered, other)],
                axis=1 + done,
            )
        return gathered.reshape(count, self.size * rows, width)

    def scatter_sum(self, values):
        count, rows, width = values.shape
        rows //= self.size
        summed = values
        for bit in range(self.bits):
            summed = summed.reshape(count, self.size >> (bit + 1), 2, rows, width)
            upper = ((self.index >> bit) & 1) == 1
            low, high = summed[:, :, 0], summed[:, :, 1]
            summed = jnp.where(upper, high, low) + self.swap(jnp.where(upper, low, high), bit)
        return summed.reshape(count, rows, width)


def split_float(values):
    pieces = []
    for _ in range(3):
        piece = lax.reduce_precision(values, 8, 7)
        pieces.append(piece.astype(BF16))
        values = values - piece
    return pieces


def attention_kernel(len_ref, q_ref, kn_ref, vn_ref, ck_ref, cv_ref, o_ref, kbuf, vbuf, sbuf, sems):
    width = q_ref.shape[1]
    tiles = width // LANE
    scale = 1.0 / math.sqrt(DH)
    lanes = lax.broadcasted_iota(jnp.int32, (NEW, 2 * LANE), 1)
    rows = lax.broadcasted_iota(jnp.int32, (2 * NEW, NEW), 0)
    cols = lax.broadcasted_iota(jnp.int32, (2 * NEW, NEW), 1)
    causal = cols <= jnp.where(rows >= NEW, rows - NEW, rows)

    def run(length):
        step = min(KEYS, length)

        def copy(which, tile):
            source, target = ((ck_ref, kbuf), (cv_ref, vbuf))[which]
            at = pl.ds(tile * LANE, LANE)
            return pltpu.make_async_copy(
                source.at[0, pl.ds(0, length), at],
                target.at[pl.ds(0, length), at],
                sems.at[which, tile],
            )

        for first in range(0, tiles, 2):
            for which in range(2):
                for tile in range(first, min(first + 2, tiles)):
                    copy(which, tile).start()
        arrived = set()

        def need(which, tile):
            if (which, tile) not in arrived:
                arrived.add((which, tile))
                copy(which, tile).wait()

        for group in range(width // GROUP):
            for half in range(2):
                tile = group * 3 + half
                window = pl.ds(tile * LANE, 2 * LANE)
                first_col = 64 * half
                in_a = (lanes >= first_col) & (lanes < first_col + DH)
                in_b = (lanes >= first_col + DH) & (lanes < first_col + 2 * DH)
                q_window = q_ref[:, window].astype(F32)
                pair = jnp.concatenate(
                    [jnp.where(in_a, q_window, 0.0), jnp.where(in_b, q_window, 0.0)], axis=0
                ).astype(BF16)

                def score(keys):
                    return (
                        lax.dot_general(
                            pair, keys, (((1,), (1,)), ((), ())), preferred_element_type=F32
                        )
                        * scale
                    )

                fresh = jnp.where(causal, score(kn_ref[:, window]), -1e30)
                need(0, tile)
                need(0, tile + 1)
                top = fresh
                for start in range(0, length, step):
                    scores = score(kbuf[pl.ds(start, step), window])
                    sbuf[:, pl.ds(start, step)] = scores
                    for lane in range(0, step, LANE):
                        top = jnp.maximum(top, scores[:, lane : lane + LANE])
                highest = jnp.max(top, axis=1, keepdims=True)
                weights = jnp.exp(fresh - highest)
                total = weights
                mixed = jnp.dot(
                    weights.astype(BF16), vn_ref[:, window], preferred_element_type=F32
                )
                need(1, tile)
                need(1, tile + 1)
                for start in range(0, length, step):
                    weights = jnp.exp(sbuf[:, pl.ds(start, step)] - highest)
                    for lane in range(0, step, LANE):
                        total = total + weights[:, lane : lane + LANE]
                    mixed = mixed + jnp.dot(
                        weights.astype(BF16),
                        vbuf[pl.ds(start, step), window],
                        preferred_element_type=F32,
                    )
                mixed = mixed / jnp.sum(total, axis=1, keepdims=True)
                before = o_ref[:, window].astype(F32) if half else 0.0
                o_ref[:, window] = jnp.where(
                    in_a, mixed[:NEW], jnp.where(in_b, mixed[NEW:], before)
                ).astype(BF16)

    long = len_ref[0] > SHORT

    @pl.when(long)
    def _():
        run(CACHE)

    @pl.when(jnp.logical_not(long))
    def _():
        run(SHORT)


def attend(queries, key_new, value_new, cache_keys, cache_values, cached_len):
    width = queries.shape[1]
    vmem = pl.BlockSpec(memory_space=pltpu.VMEM)
    hbm = pl.BlockSpec(memory_space=pl.ANY)
    return pl.pallas_call(
        attention_kernel,
        out_shape=jax.ShapeDtypeStruct((NEW, width), BF16),
        in_specs=[pl.BlockSpec(memory_space=pltpu.SMEM), vmem, vmem, vmem, hbm, hbm],
        out_specs=vmem,
        scratch_shapes=[
            pltpu.VMEM((CACHE, width), BF16),
            pltpu.VMEM((CACHE, width), BF16),
            pltpu.VMEM((2 * NEW, CACHE), F32),
            pltpu.SemaphoreType.DMA((2, width // LANE)),
        ],
        compiler_params=pltpu.CompilerParams(vmem_limit_bytes=40 * 1024 * 1024),
        cost_estimate=pl.CostEstimate(
            flops=8 * NEW * CACHE * width,
            bytes_accessed=4 * CACHE * width,
            transcendentals=NEW * CACHE * width // DH,
        ),
    )(cached_len, queries, key_new, value_new, cache_keys, cache_values)


def rotation_tables(cached_len, width):
    half = ROT // 2
    feature = np.arange(width) % DH
    exponent = jnp.arange(half, dtype=F32) * (2.0 / ROT)
    frequency = jnp.power(10000.0, -exponent)
    frequency = frequency[jnp.asarray(feature % half)]
    position = cached_len.astype(F32) + jnp.arange(NEW, dtype=F32)
    angle = position[:, None] * frequency[None, :]
    lower, upper = feature < half, (feature >= half) & (feature < ROT)
    cosine = jnp.where(jnp.asarray(lower | upper), jnp.cos(angle), 1.0)
    sine = jnp.sin(angle)
    from_above = jnp.where(jnp.asarray(lower), -sine, 0.0)
    from_below = jnp.where(jnp.asarray(upper), sine, 0.0)
    return cosine, from_above, from_below


def rotate(values, tables):
    cosine, from_above, from_below = tables
    half = ROT // 2
    above = jnp.roll(values, -half, axis=1)
    below = jnp.roll(values, half, axis=1)
    return values * cosine + above * from_above + below * from_below


def body(
    req_size,
    head_size,
    hidden,
    attn_norm_gain,
    attn_norm_bias,
    mlp_norm_gain,
    mlp_norm_bias,
    qkv_weight,
    qkv_bias,
    out_weight,
    out_bias,
    up_weight,
    up_bias,
    down_weight,
    down_bias,
    cache_keys,
    cache_values,
    cached_len,
):
    ring, cube = Ring(req_size), Cube(head_size)
    half_way = req_size // 2
    tokens, model = hidden.shape
    part = model // req_size
    mine = tokens // head_size
    width = qkv_weight.shape[1] // 3
    local_heads = width // DH
    req_index = lax.axis_index("req")

    def my_part(vector):
        return lax.dynamic_slice_in_dim(vector, req_index * part, part, 0)

    rows = lax.dynamic_slice_in_dim(hidden, cube.index * mine, mine, 0)
    widened = rows.astype(F32)
    center = jnp.mean(widened, axis=-1, keepdims=True)
    spread = jnp.mean(jnp.square(widened - center), axis=-1, keepdims=True)
    pieces = split_float(center) + split_float(lax.rsqrt(spread + 1e-05))
    stats = jnp.pad(jnp.concatenate(pieces, axis=1), ((0, 0), (0, LANE - len(pieces))))

    def message(distance):
        features = lax.dynamic_slice_in_dim(rows, ring.block(distance) * part, part, 1)
        return jnp.concatenate([features, stats], axis=1)

    def receive(distance):
        if distance == 0:
            return message(0)
        return ring.shift(message(-distance), -distance)

    gains = [my_part(v) for v in (attn_norm_gain, attn_norm_bias, mlp_norm_gain, mlp_norm_bias)]
    residual, attn_normed, mlp_normed = {}, {}, {}
    near = [d for d in range(1 - half_way, half_way) if abs(d) < half_way - 1]
    for group in ([half_way, half_way - 1, 1 - half_way], near):
        own = [receive(d) for d in group]
        for d, rows_of in zip(group, own):
            residual[d] = rows_of[:, :part]
        full = cube.gather(jnp.stack(own)).astype(F32)
        values, numbers = full[..., :part], full[..., part:]
        center_of = numbers[..., 0:1] + numbers[..., 1:2] + numbers[..., 2:3]
        scale_of = numbers[..., 3:4] + numbers[..., 4:5] + numbers[..., 5:6]
        normal = (values - center_of) * scale_of
        attn = (normal * gains[0] + gains[1]).astype(BF16)
        mlp = (normal * gains[2] + gains[3]).astype(BF16)
        for i, d in enumerate(group):
            attn_normed[d], mlp_normed[d] = attn[i], mlp[i]

    def columns(array, which):
        return jnp.concatenate(
            [
                array[..., (3 * h + w) * DH : (3 * h + w + 1) * DH]
                for w in which
                for h in range(local_heads)
            ],
            axis=-1,
        )

    q_weight, kv_weight = columns(qkv_weight, (0,)), columns(qkv_weight, (1, 2))

    def q_term(d):
        return jnp.dot(attn_normed[d], q_weight, preferred_element_type=F32)

    def kv_term(d):
        return jnp.dot(attn_normed[d], kv_weight, preferred_element_type=F32)

    def up_term(d):
        return jnp.dot(mlp_normed[d], up_weight, preferred_element_type=F32)

    def reduce(term, dtype, forward_steps):
        total = term(0)
        for sign, steps in ((1, forward_steps), (-1, req_size - 1 - forward_steps)):
            running = term(half_way if steps == half_way else sign * steps).astype(dtype)
            for step in range(steps):
                running = ring.shift(running, sign)
                left = steps - 1 - step
                if left:
                    running = (running.astype(F32) + term(sign * left)).astype(dtype)
            total = total + running.astype(F32)
        return total

    up_sum = reduce(up_term, BF16, half_way) + up_bias
    q_sum = reduce(q_term, F32, half_way - 1) + columns(qkv_bias, (0,))
    kv_sum = reduce(kv_term, BF16, half_way - 1) + columns(qkv_bias, (1, 2))

    units = jax.nn.gelu(up_sum, approximate=True).astype(BF16)
    tables = rotation_tables(cached_len, width)
    queries = rotate(q_sum, tables).astype(BF16)
    key_rows = rotate(kv_sum[:, :width], tables).astype(BF16)
    value_rows = kv_sum[:, width:].astype(BF16)
    attended = attend(queries, key_rows, value_rows, cache_keys, cache_values, cached_len)

    cut = -(-(units.shape[1] + width) // (2 * LANE)) * LANE
    partial = {}

    def spread_out(block, weight, forward_steps):
        def use(d, arrived):
            term = jnp.dot(arrived, weight, preferred_element_type=F32)
            partial[d] = partial[d] + term if d in partial else term

        use(0, block)
        for sign, steps in ((1, forward_steps), (-1, req_size - 1 - forward_steps)):
            moving = block
            for step in range(1, steps + 1):
                moving = ring.shift(moving, sign)
                use(half_way if step == half_way else -sign * step, moving)

    spread_out(units[:, :cut], down_weight[:cut], half_way)
    spread_out(units[:, cut:], down_weight[cut:], half_way - 1)
    spread_out(attended, out_weight, half_way - 1)

    bias = my_part(out_bias) + my_part(down_bias)
    result = jnp.zeros((tokens, model), BF16)
    early = [d for d in range(1 - half_way, half_way) if abs(d) < half_way - 1]
    for group in (early, [half_way - 1, 1 - half_way], [half_way]):
        summed = cube.scatter_sum(jnp.stack([partial[d] for d in group]))
        kept = jnp.stack([residual[d] for d in group]).astype(F32)
        rows_out = (kept + summed + bias).astype(BF16)
        home = [ring.shift(rows_out[i], d) if d else rows_out[i] for i, d in enumerate(group)]
        pieces = cube.gather(jnp.stack(home))
        for i, d in enumerate(group):
            result = lax.dynamic_update_slice_in_dim(
                result, pieces[i], ring.block(-d) * part, 1
            )
    return result, key_rows[None], value_rows[None]


def solution(mesh):
    return jax.shard_map(
        functools.partial(body, mesh.shape["req"], mesh.shape["head"]),
        mesh=mesh,
        in_specs=(
            P("req", None),
            P(),
            P(),
            P(),
            P(),
            P("req", "head"),
            P("head"),
            P("head", "req"),
            P(),
            P("req", "head"),
            P("head"),
            P("head", "req"),
            P(),
            P("req", None, "head"),
            P("req", None, "head"),
            P("req"),
        ),
        out_specs=(P("req", None), P("req", None, "head"), P("req", None, "head")),
        check_vma=False,
    )
```

```python
import functools
import math

import jax
import jax.numpy as jnp
import numpy as np
from jax import lax
from jax.experimental import pallas as pl
from jax.experimental.pallas import tpu as pltpu
from jax.sharding import PartitionSpec as P

DH = 96
ROT = 24
NEW = 128
CACHE = 4096
SHORT = 128
GROUP = 4 * DH
LANE = 128
KEYS = 512
CHUNK = 384
F32 = jnp.float32
BF16 = jnp.bfloat16
MIB = 1024 * 1024


def ring_order(size):
    inner = 1
    while 4 * inner * inner <= size:
        inner *= 2
    outer = size // inner
    order = [a * inner for a in range(outer)]
    forward = True
    for a in reversed(range(outer)):
        row = list(range(1, inner))
        order += [a * inner + b for b in (row if forward else row[::-1])]
        forward = not forward
    return order


def pick(table, index):
    value = jnp.int32(table[0])
    for i in range(1, len(table)):
        value = jnp.where(index == i, jnp.int32(table[i]), value)
    return value


def block_at(order, distance):
    size = len(order)
    here = lax.axis_index("req")
    return pick([order[(order.index(i) + distance) % size] for i in range(size)], here)


ANYWHERE = pl.BlockSpec(memory_space=pl.ANY)
ON_CHIP = pl.BlockSpec(memory_space=pltpu.VMEM)


def call(kernel, outs, args, scratch=(), flops=0, limit=32):
    args = [a if isinstance(a, tuple) else (a, ON_CHIP) for a in args]
    return pl.pallas_call(
        kernel,
        out_shape=[jax.ShapeDtypeStruct(*o) for o in outs],
        in_specs=[spec for _, spec in args],
        out_specs=[ON_CHIP] * len(outs),
        scratch_shapes=list(scratch),
        compiler_params=pltpu.CompilerParams(vmem_limit_bytes=limit * MIB),
        cost_estimate=pl.CostEstimate(
            flops=flops,
            bytes_accessed=sum(math.prod(shape) * 4 for shape, _ in outs),
            transcendentals=0,
        ),
    )(*(a for a, _ in args))


def anywhere(*arrays):
    return [(a, ANYWHERE) for a in arrays]


def fetch(pairs, semaphores, first=0):
    copies = [
        pltpu.make_async_copy(source, target, semaphores.at[first + i])
        for i, (source, target) in enumerate(pairs)
    ]
    for copy in copies:
        copy.start()
    return copies


def wait(copies):
    for copy in copies:
        copy.wait()


def rows_pairs(pieces, index, raw):
    head = lax.axis_index("head")
    rows = raw.shape[0] // len(pieces)
    return [
        (
            piece.at[pl.ds(index * rows, rows), :],
            raw.at[pl.ds(pl.multiple_of((head ^ mask) * rows, rows), rows), :],
        )
        for mask, piece in enumerate(pieces)
    ]


def wide(ref, first, count):
    return jnp.concatenate([ref[i : i + 1, :] for i in range(first, first + count)], axis=1)


def split_float(values, count):
    pieces = []
    for _ in range(count):
        piece = values.astype(BF16)
        pieces.append(piece)
        values = values - piece.astype(F32)
    return pieces


def message_kernel(order, distances, hidden_ref, *refs):
    outs, (buffer, semaphore) = refs[-2 - len(distances) : -2], refs[-2:]
    rows, width = outs[0].shape
    part = width - LANE
    mine = pl.ds(pl.multiple_of(lax.axis_index("head") * rows, rows), rows)
    copy = pltpu.make_async_copy(hidden_ref.at[mine, :], buffer, semaphore)
    copy.start()
    copy.wait()
    widened = buffer[...].astype(F32)
    center = jnp.mean(widened, axis=-1, keepdims=True)
    spread = jnp.mean(jnp.square(widened - center), axis=-1, keepdims=True)
    pieces = split_float(center, 3) + split_float(lax.rsqrt(spread + 1e-05), 3)
    lanes = lax.broadcasted_iota(jnp.int32, (rows, LANE), 1)
    stats = jnp.zeros((rows, LANE), F32)
    for i, piece in enumerate(pieces):
        stats = jnp.where(lanes == i, piece.astype(F32), stats)
    stats = stats.astype(BF16)
    for out, distance in zip(outs, distances):
        first = pl.multiple_of(block_at(order, -distance) * part, LANE)
        out[:, :part] = buffer[:, pl.ds(first, part)]
        out[:, part:] = stats


def stack_kernel(count, *refs):
    out = refs[-1]
    rows = out.shape[0] // count
    for i in range(count):
        out[i * rows : (i + 1) * rows, :] = refs[i][...]


def reordered(values):
    return jnp.concatenate(
        [
            values[:, (3 * h + kind) * DH : (3 * h + kind + 1) * DH]
            for kind in range(3)
            for h in range(GROUP // DH)
        ],
        axis=1,
    )


def prepare_kernel(weight_ref, *refs):
    out = refs[-1]
    span = 3 * GROUP
    for c in range(weight_ref.shape[1] // span):
        at = pl.ds(c * span, span)

        def strip(r, _, at=at):
            rows = pl.ds(pl.multiple_of(r * 64, 64), 64)
            out[rows, at] = reordered(weight_ref[rows, at])
            return 0

        lax.fori_loop(0, weight_ref.shape[0] // 64, strip, 0)


def local_kernel(bias, *refs):
    vectors, (bias_out, local_ref) = refs[:6], refs[-2:]
    span = 3 * GROUP
    for c in range(bias_out.shape[1] // span):
        row = wide(bias, c * span // LANE, span // LANE)
        bias_out[:, pl.ds(c * span, span)] = reordered(jnp.broadcast_to(row, (8, span)))[0:1]
    part = local_ref.shape[1]
    first = lax.axis_index("req") * (part // LANE)
    for i in range(part // LANE):
        at = pl.ds(i * LANE, LANE)
        rows_of = [v[pl.ds(first + i, 1), :] for v in vectors]
        for j in range(4):
            local_ref[j : j + 1, at] = rows_of[j]
        local_ref[4:5, at] = rows_of[4] + rows_of[5]
        local_ref[5:8, at] = jnp.zeros((3, LANE), F32)


def normed(raw, local_ref, first):
    part = raw.shape[1] - LANE
    stats = raw[:, part:].astype(F32)
    center = stats[:, 0:1] + stats[:, 1:2] + stats[:, 2:3]
    scale = stats[:, 3:4] + stats[:, 4:5] + stats[:, 5:6]
    normal = (raw[:, :part].astype(F32) - center) * scale
    return (
        normal * local_ref[first : first + 1, :] + local_ref[first + 1 : first + 2, :]
    ).astype(BF16)


def up_chunks(width):
    return [(pl.ds(c, CHUNK), pl.ds(c, CHUNK)) for c in range(0, width, CHUNK)]


def up_emit(values, old, _):
    if old is not None:
        values = values + old.astype(F32)
    return values.astype(BF16)


def qkv_chunks(width):
    chunks = []
    for c in range(width // (3 * GROUP)):
        source, target = 3 * c * GROUP, 4 * c * GROUP
        chunks.append((pl.ds(source, GROUP), pl.ds(target, 2 * GROUP)))
        chunks.append((pl.ds(source + GROUP, 2 * GROUP), pl.ds(target + 2 * GROUP, 2 * GROUP)))
    return chunks


def qkv_emit(values, old, source):
    if source.size == 2 * GROUP:
        return up_emit(values, old, source)
    if old is not None:
        values = values + old[:, :GROUP].astype(F32) + old[:, GROUP:].astype(F32)
    return jnp.concatenate(split_float(values, 2), axis=1)


def far_kernel(chunks, emit, first, index, masks, *refs):
    pieces, (local_ref, weight_ref, _) = refs[:masks], refs[masks : masks + 3]
    forward, backward, raw, local, semaphores = refs[masks + 3 :]
    wait(fetch([(local_ref, local)] + rows_pairs(pieces, index, raw.at[0]), semaphores))
    block = normed(raw.at[0], local, first)
    half = forward.shape[1]
    for source, target in chunks(weight_ref.shape[1]):
        product = jnp.dot(block, weight_ref[:, source], preferred_element_type=F32)
        out, begin = (forward, 0) if target.start < half else (backward, half)
        out[:, pl.ds(target.start - begin, target.size)] = emit(product, None, source)


def step_kernel(chunks, emit, first, indices, masks, *refs):
    pieces = [refs[b * masks : (b + 1) * masks] for b in range(2)]
    local_ref, weight_ref, *received, _ = refs[2 * masks : 2 * masks + 5]
    *outs, raw, local, semaphores = refs[2 * masks + 5 :]
    pairs = [(local_ref, local)]
    for b, index in enumerate(indices):
        pairs += rows_pairs(pieces[b], index, raw.at[b])
    wait(fetch(pairs, semaphores))
    stacked = jnp.concatenate([normed(raw.at[b], local, first) for b in range(2)], axis=0)
    for source, target in chunks(weight_ref.shape[1]):
        product = jnp.dot(stacked, weight_ref[:, source], preferred_element_type=F32)
        for i, (out, old) in enumerate(zip(outs, received)):
            width = old.shape[1]
            begin = i * (out.shape[1] - width)
            here = begin <= target.start < begin + width
            out[:, target] = emit(
                product[i * NEW : (i + 1) * NEW],
                old[:, pl.ds(target.start - begin, target.size)] if here else None,
                source,
            )


def units_kernel(index, masks, *refs):
    pieces = refs[:masks]
    local_ref, weight_ref, bias_ref, plus, minus, attended, out = refs[masks : masks + 7]
    raw, local, bias, semaphores = refs[masks + 7 :]
    pairs = [(local_ref, local), (bias_ref, bias)] + rows_pairs(pieces, index, raw.at[0])
    wait(fetch(pairs, semaphores))
    block = normed(raw.at[0], local, 2)
    width = weight_ref.shape[1]
    for at, _ in up_chunks(width):
        total = jnp.dot(block, weight_ref[:, at], preferred_element_type=F32)
        total = total + wide(bias, at.start // LANE, CHUNK // LANE)
        total = total + plus[:, at].astype(F32) + minus[:, at].astype(F32)
        out[:, at] = jax.nn.gelu(total, approximate=True).astype(BF16)
    out[:, width:] = attended[...]


def heads_kernel(index, masks, *refs):
    pieces = refs[:masks]
    local_ref, weight_ref, bias_ref, *table_refs = refs[masks : masks + 6]
    plus, minus, _, q_out, k_out, v_out, raw, local, bias, tables, semaphores = refs[masks + 6 :]
    pairs = [(local_ref, local), (bias_ref, bias)] + rows_pairs(pieces, index, raw.at[0])
    pairs += [(ref, tables.at[i]) for i, ref in enumerate(table_refs)]
    wait(fetch(pairs, semaphores))
    block = normed(raw.at[0], local, 0)
    half = ROT // 2
    cosine, from_above, from_below = tables[0], tables[1], tables[2]

    def rotate(values):
        above = pltpu.roll(values, GROUP - half, 1)
        below = pltpu.roll(values, half, 1)
        return (values * cosine + above * from_above + below * from_below).astype(BF16)

    for c in range(weight_ref.shape[1] // (3 * GROUP)):
        source = pl.ds(3 * c * GROUP, 3 * GROUP)
        total = jnp.dot(block, weight_ref[:, source], preferred_element_type=F32)
        total = total + bias[:, source]
        query, key, value = (total[:, i * GROUP : (i + 1) * GROUP] for i in range(3))
        for other in (plus, minus):
            high, low, other_key, other_value = (
                other[:, (4 * c + i) * GROUP : (4 * c + i + 1) * GROUP].astype(F32)
                for i in range(4)
            )
            query, key, value = query + high + low, key + other_key, value + other_value
        at = pl.ds(c * GROUP, GROUP)
        q_out[:, at] = rotate(query)
        k_out[:, at] = rotate(key)
        v_out[:, at] = value.astype(BF16)


def attention_kernel(
    len_ref, q_hbm, kn_hbm, vn_hbm, ck_ref, cv_ref, _, o_ref, rows, kbuf, vbuf, sbuf, sems, row_sems
):
    width = o_ref.shape[1]
    tiles = width // LANE
    q_ref, kn_ref, vn_ref = rows.at[0], rows.at[1], rows.at[2]
    early = fetch([(q_hbm, q_ref), (kn_hbm, kn_ref), (vn_hbm, vn_ref)], row_sems)
    scale = 1.0 / math.sqrt(DH)
    lanes = lax.broadcasted_iota(jnp.int32, (NEW, 2 * LANE), 1)
    rows = lax.broadcasted_iota(jnp.int32, (2 * NEW, NEW), 0)
    cols = lax.broadcasted_iota(jnp.int32, (2 * NEW, NEW), 1)
    causal = cols <= jnp.where(rows >= NEW, rows - NEW, rows)

    def run(length):
        step = min(KEYS, length)

        def copy(which, tile):
            source, target = ((ck_ref, kbuf), (cv_ref, vbuf))[which]
            at = pl.ds(tile * LANE, LANE)
            return pltpu.make_async_copy(
                source.at[0, pl.ds(0, length), at],
                target.at[pl.ds(0, length), at],
                sems.at[which, tile],
            )

        for first in range(0, tiles, 2):
            for which in range(2):
                for tile in range(first, min(first + 2, tiles)):
                    copy(which, tile).start()
        arrived = set()
        wait(early)

        def need(which, tile):
            if (which, tile) not in arrived:
                arrived.add((which, tile))
                copy(which, tile).wait()

        for group in range(width // GROUP):
            for half in range(2):
                tile = group * 3 + half
                window = pl.ds(tile * LANE, 2 * LANE)
                first_col = 64 * half
                in_a = (lanes >= first_col) & (lanes < first_col + DH)
                in_b = (lanes >= first_col + DH) & (lanes < first_col + 2 * DH)
                q_window = q_ref[:, window].astype(F32)
                pair = jnp.concatenate(
                    [jnp.where(in_a, q_window, 0.0), jnp.where(in_b, q_window, 0.0)], axis=0
                ).astype(BF16)

                def score(keys):
                    return (
                        lax.dot_general(
                            pair, keys, (((1,), (1,)), ((), ())), preferred_element_type=F32
                        )
                        * scale
                    )

                fresh = jnp.where(causal, score(kn_ref[:, window]), -1e30)
                need(0, tile)
                need(0, tile + 1)
                top = fresh
                for start in range(0, length, step):
                    scores = score(kbuf[pl.ds(start, step), window])
                    sbuf[:, pl.ds(start, step)] = scores
                    for lane in range(0, step, LANE):
                        top = jnp.maximum(top, scores[:, lane : lane + LANE])
                highest = jnp.max(top, axis=1, keepdims=True)
                weights = jnp.exp(fresh - highest)
                total = weights
                mixed = jnp.dot(
                    weights.astype(BF16), vn_ref[:, window], preferred_element_type=F32
                )
                need(1, tile)
                need(1, tile + 1)
                for start in range(0, length, step):
                    weights = jnp.exp(sbuf[:, pl.ds(start, step)] - highest)
                    for lane in range(0, step, LANE):
                        total = total + weights[:, lane : lane + LANE]
                    mixed = mixed + jnp.dot(
                        weights.astype(BF16),
                        vbuf[pl.ds(start, step), window],
                        preferred_element_type=F32,
                    )
                mixed = mixed / jnp.sum(total, axis=1, keepdims=True)
                before = o_ref[:, window].astype(F32) if half else 0.0
                o_ref[:, window] = jnp.where(
                    in_a, mixed[:NEW], jnp.where(in_b, mixed[NEW:], before)
                ).astype(BF16)

    long = len_ref[0] > SHORT

    @pl.when(long)
    def _():
        run(CACHE)

    @pl.when(jnp.logical_not(long))
    def _():
        run(SHORT)


def attend(queries, key_new, value_new, cache_keys, cache_values, cached_len, after):
    width = queries.shape[1]
    (attended,) = call(
        attention_kernel,
        [((NEW, width), BF16)],
        [
            (cached_len, pl.BlockSpec(memory_space=pltpu.SMEM)),
            *anywhere(queries, key_new, value_new, cache_keys, cache_values, after),
        ],
        [
            pltpu.VMEM((3, NEW, width), BF16),
            pltpu.VMEM((CACHE, width), BF16),
            pltpu.VMEM((CACHE, width), BF16),
            pltpu.VMEM((2 * NEW, CACHE), F32),
            pltpu.SemaphoreType.DMA((2, width // LANE)),
            pltpu.SemaphoreType.DMA((3,)),
        ],
        flops=8 * NEW * CACHE * width,
        limit=50,
    )
    return attended


def rotation_tables(cached_len):
    half = ROT // 2
    feature = np.arange(GROUP) % DH
    exponent = jnp.asarray((feature % half).astype(np.float32)) * (2.0 / ROT)
    frequency = jnp.power(10000.0, -exponent)
    position = cached_len.astype(F32) + jnp.arange(NEW, dtype=F32)
    angle = position[:, None] * frequency[None, :]
    lower, upper = jnp.asarray(feature < half), jnp.asarray((feature >= half) & (feature < ROT))
    cosine, sine = jnp.cos(angle), jnp.sin(angle)
    return (
        jnp.where(lower | upper, cosine, 1.0),
        jnp.where(lower, -sine, 0.0),
        jnp.where(upper, sine, 0.0),
    )


def cut_kernel(left_ref, right_ref, left, right):
    left[...] = left_ref[:, : left.shape[1]]
    right[...] = right_ref[:, left.shape[1] :]


def gather_weights_kernel(down_ref, out_ref, _, weights, semaphores):
    rows = down_ref.shape[0]
    wait(
        fetch(
            [
                (down_ref, weights.at[pl.ds(0, rows), :]),
                (out_ref, weights.at[pl.ds(rows, out_ref.shape[0]), :]),
            ],
            semaphores,
        )
    )


def out_kernel(layout, rows, masks, weights, *refs):
    inputs, outs, total = list(refs), refs[-1 - masks : -1], refs[-1]
    head = lax.axis_index("head")
    for i, pieces in enumerate(layout):
        term = None
        for begin in pieces:
            ref = inputs.pop(0)
            product = jnp.dot(
                ref[...], weights[pl.ds(begin, ref.shape[1]), :], preferred_element_type=F32
            )
            term = product if term is None else term + product
        total[...] = term
        for mask, out in enumerate(outs):
            at = pl.ds(pl.multiple_of((head ^ mask) * rows, rows), rows)
            out[i * rows : (i + 1) * rows, :] = total[at, :]


def final_kernel(count, indices, *refs):
    terms, (residual_ref, local_ref) = refs[:count], refs[count : count + 2]
    outs, (residual, local, semaphores) = refs[-3 - len(indices) : -3], refs[-3:]
    rows, part = outs[0].shape
    pairs = [(local_ref, local)]
    for i, index in enumerate(indices):
        pairs.append((residual_ref.at[pl.ds(index * rows, rows), :], residual.at[i]))
    wait(fetch(pairs, semaphores))
    for i, out in enumerate(outs):
        total = residual[i][:, :part].astype(F32)
        for term in terms:
            total = total + term[i * rows : (i + 1) * rows, :]
        out[...] = (total + local[4:5, :]).astype(BF16)


def assemble_kernel(order, batches, rows, masks, *refs):
    out, refs = refs[-1], list(refs[:-1])
    part = refs[0].shape[1]
    head = lax.axis_index("head")
    for batch in batches:
        for mask in range(masks):
            piece = refs.pop(0)
            at = pl.ds(pl.multiple_of((head ^ mask) * rows, rows), rows)
            for i, distance in enumerate(batch):
                first = pl.multiple_of(block_at(order, -distance) * part, LANE)
                out[at, pl.ds(first, part)] = piece[i * rows : (i + 1) * rows, :]


def body(
    req_size,
    head_size,
    hidden,
    attn_norm_gain,
    attn_norm_bias,
    mlp_norm_gain,
    mlp_norm_bias,
    qkv_weight,
    qkv_bias,
    out_weight,
    out_bias,
    up_weight,
    up_bias,
    down_weight,
    down_bias,
    cache_keys,
    cache_values,
    cached_len,
):
    order = ring_order(req_size)
    far = req_size // 2
    tokens, model = hidden.shape
    part = model // req_size
    rows = tokens // head_size
    bits = head_size.bit_length() - 1
    qkv_width, up_width = qkv_weight.shape[1], up_weight.shape[1]
    width = qkv_width // 3
    heads = qkv_width // (3 * GROUP)

    def shift(values, distance):
        pairs = [(order[i], order[(i + distance) % req_size]) for i in range(req_size)]
        return lax.ppermute(values, "req", pairs)

    def swap(values, mask):
        return lax.ppermute(values, "head", [(i, i ^ mask) for i in range(head_size)])

    def straight(values, distance, mask):
        pairs = [
            (order[i] * head_size + h, order[(i + distance) % req_size] * head_size + (h ^ mask))
            for i in range(req_size)
            for h in range(head_size)
        ]
        return lax.ppermute(values, ("req", "head"), pairs)

    def exchange(values):
        held = {0: values}
        for bit in reversed(range(bits)):
            for mask in sorted(held):
                held[mask | 1 << bit] = swap(held[mask], 1 << bit)
        return [held[mask] for mask in range(head_size)]

    distances = list(range(1 - far, far + 1))
    outer = [far, far - 1, 1 - far]
    inner = [d for d in distances if d not in outer]

    wanted = outer + inner
    sent = call(
        functools.partial(message_kernel, order, wanted),
        [((rows, part + LANE), BF16)] * len(wanted),
        anywhere(hidden),
        [pltpu.VMEM((rows, model), BF16), pltpu.SemaphoreType.DMA],
        limit=56,
    )
    got = [shift(m, -d) if d else m for m, d in zip(sent, wanted)]

    def stacked(blocks, after=()):
        (result,) = call(
            functools.partial(stack_kernel, len(blocks)),
            [((len(blocks) * blocks[0].shape[0], blocks[0].shape[1]), BF16)],
            [*blocks, *anywhere(*after)],
        )
        return result

    vectors = [
        v.reshape(-1, LANE)
        for v in (attn_norm_gain, attn_norm_bias, mlp_norm_gain, mlp_norm_bias, out_bias, down_bias)
    ]
    tables = rotation_tables(cached_len)
    (heads_weight,) = call(
        prepare_kernel,
        [((part, qkv_width), BF16)],
        [qkv_weight, *anywhere(tables[0], sent[0])],
        flops=2 * part * qkv_width * GROUP,
    )
    outer_stack = stacked(got[: len(outer)], [heads_weight, *got[len(outer) :]])
    heads_bias, local = call(
        local_kernel,
        [((1, qkv_width), F32), ((8, part), F32)],
        [qkv_bias.reshape(-1, LANE), *vectors, *anywhere(outer_stack)],
    )
    inner_stack = stacked(got[len(outer) :])
    groups = [exchange(outer_stack), exchange(inner_stack)]
    places = {d: (g, i) for g, group in enumerate((outer, inner)) for i, d in enumerate(group)}

    def pieces_of(d):
        return anywhere(*groups[places[d][0]])

    def buffers(count, *more):
        return [
            pltpu.VMEM((count, NEW, part + LANE), BF16),
            pltpu.VMEM((8, part), F32),
            *more,
            pltpu.SemaphoreType.DMA((count * head_size + 5,)),
        ]

    kinds = [
        (qkv_chunks, qkv_emit, 0, heads_weight, 4 * GROUP * heads),
        (up_chunks, up_emit, 2, up_weight, up_width),
    ]
    moving = [None, None]
    after = inner_stack
    for left in range(far, 0, -1):
        for kind, (chunks, emit, first, weight, out_width) in enumerate(kinds):
            if left == far:
                results = call(
                    functools.partial(far_kernel, chunks, emit, first, places[far][1], head_size),
                    [((NEW, out_width // 2), BF16)] * 2,
                    [*pieces_of(far), *anywhere(local), weight, *anywhere(after)],
                    buffers(1),
                    flops=2 * NEW * weight.size,
                )
            else:
                indices = [places[left][1], places[-left][1]]
                results = call(
                    functools.partial(step_kernel, chunks, emit, first, indices, head_size),
                    [((NEW, out_width), BF16)] * 2,
                    [
                        *pieces_of(left),
                        *pieces_of(-left),
                        *anywhere(local),
                        weight,
                        *moving[kind],
                        *anywhere(after),
                    ],
                    buffers(2),
                    flops=4 * NEW * weight.size,
                )
            after = results[0]
            moving[kind] = [shift(results[0], 1), shift(results[1], -1)]

    index = places[0][1]
    queries, key_rows, value_rows = call(
        functools.partial(heads_kernel, index, head_size),
        [((NEW, width), BF16)] * 3,
        [
            *pieces_of(0),
            *anywhere(local),
            heads_weight,
            *anywhere(heads_bias, *tables),
            *moving[0],
            *anywhere(after),
        ],
        buffers(1, pltpu.VMEM((1, qkv_width), F32), pltpu.VMEM((3, NEW, GROUP), F32)),
        flops=2 * NEW * heads_weight.size,
    )
    attended = attend(
        queries, key_rows, value_rows, cache_keys, cache_values, cached_len, after
    )
    bias_rows = up_bias.reshape(-1, LANE)
    full_width = up_width + width
    (block,) = call(
        functools.partial(units_kernel, index, head_size),
        [((NEW, full_width), BF16)],
        [
            *pieces_of(0),
            *anywhere(local),
            up_weight,
            *anywhere(bias_rows),
            *moving[1],
            attended,
        ],
        buffers(1, pltpu.VMEM(bias_rows.shape, F32)),
        flops=2 * NEW * up_weight.size,
    )

    blocks = {0: block}
    for step in range(1, far):
        for sign in (1, -1):
            blocks[-sign * step] = shift(blocks[-sign * (step - 1)], sign)
    cut = full_width // (2 * LANE) * LANE
    halves = call(
        cut_kernel,
        [((NEW, cut), BF16), ((NEW, full_width - cut), BF16)],
        [blocks[1 - far], blocks[far - 1]],
    )
    far_halves = [shift(halves[0], 1), shift(halves[1], -1)]

    (out_weights,) = call(
        gather_weights_kernel,
        [((full_width, part), BF16)],
        anywhere(down_weight, out_weight, block),
        [pltpu.SemaphoreType.DMA((2,))],
    )

    def products(batch, after):
        layout = [[0, cut] if d == far else [0] for d in batch]
        args = [a for d in batch for a in (far_halves if d == far else [blocks[d]])]
        return call(
            functools.partial(out_kernel, layout, rows, head_size),
            [((len(batch) * rows, part), F32)] * head_size,
            [out_weights, *args, *anywhere(*after)],
            [pltpu.VMEM((NEW, part), F32)],
            flops=2 * len(batch) * NEW * out_weights.size,
        )

    def finish(batch, terms, after):
        indices = [places[d][1] for d in batch]
        (group,) = {places[d][0] for d in batch}
        residual = groups[group][0]
        return call(
            functools.partial(final_kernel, len(terms), indices),
            [((rows, part), BF16)] * len(batch),
            [*terms, *anywhere(residual, local, *after)],
            [
                pltpu.VMEM((len(batch), rows, part + LANE), BF16),
                pltpu.VMEM((8, part), F32),
                pltpu.SemaphoreType.DMA((len(batch) + 1,)),
            ],
        )

    def halved(terms):
        held = dict(enumerate(terms))
        for bit in range(bits):
            leaving = [m for m in held if m >> bit & 1]
            arrived = {m: swap(held[m], 1 << bit) for m in leaving}
            if bit < bits - 1:
                for m in leaving:
                    held[m ^ 1 << bit] = held[m ^ 1 << bit] + arrived[m]
                    del held[m]
        return [held[0], arrived[1 << bits - 1]]

    def homeward(ready, batch):
        return [shift(b, d) if d else b for b, d in zip(ready, batch)]

    batches = [[0, 1, -1], *([d, -d] for d in range(2, far)), [far]]
    pieces, after = [], []
    for batch in batches[:-2]:
        ready = finish(batch, halved(products(batch, after)), [])
        pieces += exchange(stacked(homeward(ready, batch)))
        after = [ready[0]]
    near, last = batches[-2:]
    near_terms = halved(products(near, [*after, halves[0]]))
    terms = products(last, [])
    ready = finish(near, near_terms, [terms[0]])
    pieces += exchange(stacked(homeward(ready, near)))
    (block,) = finish(last, [terms[0]] + [swap(terms[m], m) for m in range(1, head_size)], [])
    pieces += [straight(block, far, mask) for mask in range(head_size)]
    (result,) = call(
        functools.partial(assemble_kernel, order, batches, rows, head_size),
        [((tokens, model), BF16)],
        pieces,
    )
    return result, key_rows[None], value_rows[None]


def solution(mesh):
    return jax.shard_map(
        functools.partial(body, mesh.shape["req"], mesh.shape["head"]),
        mesh=mesh,
        in_specs=(
            P("req", None),
            P(),
            P(),
            P(),
            P(),
            P("req", "head"),
            P("head"),
            P("head", "req"),
            P(),
            P("req", "head"),
            P("head"),
            P("head", "req"),
            P(),
            P("req", None, "head"),
            P("req", None, "head"),
            P("req"),
        ),
        out_specs=(P("req", None), P("req", None, "head"), P("req", None, "head")),
        check_vma=False,
    )
```

```python
import functools
import math

import jax
import jax.numpy as jnp
import numpy as np
from jax import lax
from jax.experimental import pallas as pl
from jax.experimental.pallas import tpu as pltpu
from jax.sharding import PartitionSpec as P

DH = 96
ROT = 24
NEW = 128
CACHE = 4096
SHORT = 128
GROUP = 4 * DH
LANE = 128
KEYS = 512
CHUNK = 384
F32 = jnp.float32
BF16 = jnp.bfloat16
MIB = 1024 * 1024


def ring_order(size):
    inner = 1
    while 4 * inner * inner <= size:
        inner *= 2
    outer = size // inner
    order = [a * inner for a in range(outer)]
    forward = True
    for a in reversed(range(outer)):
        row = list(range(1, inner))
        order += [a * inner + b for b in (row if forward else row[::-1])]
        forward = not forward
    return order


def pick(table, index):
    value = jnp.int32(table[0])
    for i in range(1, len(table)):
        value = jnp.where(index == i, jnp.int32(table[i]), value)
    return value


def block_at(order, distance):
    size = len(order)
    here = lax.axis_index("req")
    return pick([order[(order.index(i) + distance) % size] for i in range(size)], here)


ANYWHERE = pl.BlockSpec(memory_space=pl.ANY)
ON_CHIP = pl.BlockSpec(memory_space=pltpu.VMEM)


def call(kernel, outs, args, scratch=(), flops=0, limit=32):
    args = [a if isinstance(a, tuple) else (a, ON_CHIP) for a in args]
    return pl.pallas_call(
        kernel,
        out_shape=[jax.ShapeDtypeStruct(*o) for o in outs],
        in_specs=[spec for _, spec in args],
        out_specs=[ON_CHIP] * len(outs),
        scratch_shapes=list(scratch),
        compiler_params=pltpu.CompilerParams(vmem_limit_bytes=limit * MIB),
        cost_estimate=pl.CostEstimate(
            flops=flops,
            bytes_accessed=sum(math.prod(shape) * 4 for shape, _ in outs),
            transcendentals=0,
        ),
    )(*(a for a, _ in args))


def anywhere(*arrays):
    return [(a, ANYWHERE) for a in arrays]


def fetch(pairs, semaphores, first=0):
    copies = [
        pltpu.make_async_copy(source, target, semaphores.at[first + i])
        for i, (source, target) in enumerate(pairs)
    ]
    for copy in copies:
        copy.start()
    return copies


def wait(copies):
    for copy in copies:
        copy.wait()


def rows_pairs(pieces, index, raw):
    head = lax.axis_index("head")
    rows = raw.shape[0] // len(pieces)
    return [
        (
            piece.at[pl.ds(index * rows, rows), :],
            raw.at[pl.ds(pl.multiple_of((head ^ mask) * rows, rows), rows), :],
        )
        for mask, piece in enumerate(pieces)
    ]


def wide(ref, first, count):
    return jnp.concatenate([ref[i : i + 1, :] for i in range(first, first + count)], axis=1)


def split_float(values, count):
    pieces = []
    for _ in range(count):
        piece = values.astype(BF16)
        pieces.append(piece)
        values = values - piece.astype(F32)
    return pieces


def message_kernel(order, distances, hidden_ref, *refs):
    outs, (buffer, semaphore) = refs[-2 - len(distances) : -2], refs[-2:]
    rows, width = outs[0].shape
    part = width - LANE
    mine = pl.ds(pl.multiple_of(lax.axis_index("head") * rows, rows), rows)
    copy = pltpu.make_async_copy(hidden_ref.at[mine, :], buffer, semaphore)
    copy.start()
    copy.wait()
    widened = buffer[...].astype(F32)
    center = jnp.mean(widened, axis=-1, keepdims=True)
    spread = jnp.mean(jnp.square(widened - center), axis=-1, keepdims=True)
    pieces = split_float(center, 3) + split_float(lax.rsqrt(spread + 1e-05), 3)
    lanes = lax.broadcasted_iota(jnp.int32, (rows, LANE), 1)
    stats = jnp.zeros((rows, LANE), F32)
    for i, piece in enumerate(pieces):
        stats = jnp.where(lanes == i, piece.astype(F32), stats)
    stats = stats.astype(BF16)
    for out, distance in zip(outs, distances):
        first = pl.multiple_of(block_at(order, -distance) * part, LANE)
        out[:, :part] = buffer[:, pl.ds(first, part)]
        out[:, part:] = stats


def stack_kernel(count, *refs):
    out = refs[-1]
    rows = out.shape[0] // count
    for i in range(count):
        out[i * rows : (i + 1) * rows, :] = refs[i][...]


def reordered(values):
    return jnp.concatenate(
        [
            values[:, (3 * h + kind) * DH : (3 * h + kind + 1) * DH]
            for kind in range(3)
            for h in range(GROUP // DH)
        ],
        axis=1,
    )


def prepare_kernel(weight_ref, *refs):
    out = refs[-1]
    span = 3 * GROUP
    for c in range(weight_ref.shape[1] // span):
        at = pl.ds(c * span, span)

        def strip(r, _, at=at):
            rows = pl.ds(pl.multiple_of(r * 64, 64), 64)
            out[rows, at] = reordered(weight_ref[rows, at])
            return 0

        lax.fori_loop(0, weight_ref.shape[0] // 64, strip, 0)


def local_kernel(bias, *refs):
    vectors, (bias_out, local_ref) = refs[:6], refs[-2:]
    span = 3 * GROUP
    for c in range(bias_out.shape[1] // span):
        row = wide(bias, c * span // LANE, span // LANE)
        bias_out[:, pl.ds(c * span, span)] = reordered(jnp.broadcast_to(row, (8, span)))[0:1]
    part = local_ref.shape[1]
    first = lax.axis_index("req") * (part // LANE)
    for i in range(part // LANE):
        at = pl.ds(i * LANE, LANE)
        rows_of = [v[pl.ds(first + i, 1), :] for v in vectors]
        for j in range(4):
            local_ref[j : j + 1, at] = rows_of[j]
        local_ref[4:5, at] = rows_of[4] + rows_of[5]
        local_ref[5:8, at] = jnp.zeros((3, LANE), F32)


def normed(raw, local_ref, first):
    part = raw.shape[1] - LANE
    stats = raw[:, part:].astype(F32)
    center = stats[:, 0:1] + stats[:, 1:2] + stats[:, 2:3]
    scale = stats[:, 3:4] + stats[:, 4:5] + stats[:, 5:6]
    normal = (raw[:, :part].astype(F32) - center) * scale
    return (
        normal * local_ref[first : first + 1, :] + local_ref[first + 1 : first + 2, :]
    ).astype(BF16)


def up_chunks(width):
    return [(pl.ds(c, CHUNK), pl.ds(c, CHUNK)) for c in range(0, width, CHUNK)]


def up_emit(values, old, _):
    if old is not None:
        values = values + old.astype(F32)
    return values.astype(BF16)


def qkv_chunks(width):
    chunks = []
    for c in range(width // (3 * GROUP)):
        source, target = 3 * c * GROUP, 4 * c * GROUP
        chunks.append((pl.ds(source, GROUP), pl.ds(target, 2 * GROUP)))
        chunks.append((pl.ds(source + GROUP, 2 * GROUP), pl.ds(target + 2 * GROUP, 2 * GROUP)))
    return chunks


def qkv_emit(values, old, source):
    if source.size == 2 * GROUP:
        return up_emit(values, old, source)
    if old is not None:
        values = values + old[:, :GROUP].astype(F32) + old[:, GROUP:].astype(F32)
    return jnp.concatenate(split_float(values, 2), axis=1)


def far_kernel(chunks, emit, first, index, masks, *refs):
    pieces, (local_ref, weight_ref, _) = refs[:masks], refs[masks : masks + 3]
    forward, backward, raw, local, semaphores = refs[masks + 3 :]
    wait(fetch([(local_ref, local)] + rows_pairs(pieces, index, raw.at[0]), semaphores))
    block = normed(raw.at[0], local, first)
    half = forward.shape[1]
    for source, target in chunks(weight_ref.shape[1]):
        product = jnp.dot(block, weight_ref[:, source], preferred_element_type=F32)
        out, begin = (forward, 0) if target.start < half else (backward, half)
        out[:, pl.ds(target.start - begin, target.size)] = emit(product, None, source)


def step_kernel(chunks, emit, first, indices, masks, *refs):
    pieces = [refs[b * masks : (b + 1) * masks] for b in range(2)]
    local_ref, weight_ref, *received, _ = refs[2 * masks : 2 * masks + 5]
    *outs, raw, local, semaphores = refs[2 * masks + 5 :]
    pairs = [(local_ref, local)]
    for b, index in enumerate(indices):
        pairs += rows_pairs(pieces[b], index, raw.at[b])
    wait(fetch(pairs, semaphores))
    stacked = jnp.concatenate([normed(raw.at[b], local, first) for b in range(2)], axis=0)
    for source, target in chunks(weight_ref.shape[1]):
        product = jnp.dot(stacked, weight_ref[:, source], preferred_element_type=F32)
        for i, (out, old) in enumerate(zip(outs, received)):
            width = old.shape[1]
            begin = i * (out.shape[1] - width)
            here = begin <= target.start < begin + width
            out[:, target] = emit(
                product[i * NEW : (i + 1) * NEW],
                old[:, pl.ds(target.start - begin, target.size)] if here else None,
                source,
            )


def units_kernel(index, masks, *refs):
    pieces = refs[:masks]
    local_ref, weight_ref, bias_ref, plus, minus, attended, out = refs[masks : masks + 7]
    raw, local, bias, semaphores = refs[masks + 7 :]
    pairs = [(local_ref, local), (bias_ref, bias)] + rows_pairs(pieces, index, raw.at[0])
    wait(fetch(pairs, semaphores))
    block = normed(raw.at[0], local, 2)
    width = weight_ref.shape[1]
    for at, _ in up_chunks(width):
        total = jnp.dot(block, weight_ref[:, at], preferred_element_type=F32)
        total = total + wide(bias, at.start // LANE, CHUNK // LANE)
        total = total + plus[:, at].astype(F32) + minus[:, at].astype(F32)
        out[:, at] = jax.nn.gelu(total, approximate=True).astype(BF16)
    out[:, width:] = attended[...]


def heads_kernel(index, masks, *refs):
    pieces = refs[:masks]
    local_ref, weight_ref, bias_ref, *table_refs = refs[masks : masks + 6]
    plus, minus, _, q_out, k_out, v_out, raw, local, bias, tables, semaphores = refs[masks + 6 :]
    pairs = [(local_ref, local), (bias_ref, bias)] + rows_pairs(pieces, index, raw.at[0])
    pairs += [(ref, tables.at[i]) for i, ref in enumerate(table_refs)]
    wait(fetch(pairs, semaphores))
    block = normed(raw.at[0], local, 0)
    half = ROT // 2
    cosine, from_above, from_below = tables[0], tables[1], tables[2]

    def rotate(values):
        above = pltpu.roll(values, GROUP - half, 1)
        below = pltpu.roll(values, half, 1)
        return (values * cosine + above * from_above + below * from_below).astype(BF16)

    for c in range(weight_ref.shape[1] // (3 * GROUP)):
        source = pl.ds(3 * c * GROUP, 3 * GROUP)
        total = jnp.dot(block, weight_ref[:, source], preferred_element_type=F32)
        total = total + bias[:, source]
        query, key, value = (total[:, i * GROUP : (i + 1) * GROUP] for i in range(3))
        for other in (plus, minus):
            high, low, other_key, other_value = (
                other[:, (4 * c + i) * GROUP : (4 * c + i + 1) * GROUP].astype(F32)
                for i in range(4)
            )
            query, key, value = query + high + low, key + other_key, value + other_value
        at = pl.ds(c * GROUP, GROUP)
        q_out[:, at] = rotate(query)
        k_out[:, at] = rotate(key)
        v_out[:, at] = value.astype(BF16)


def attention_kernel(
    len_ref, q_hbm, kn_hbm, vn_hbm, ck_ref, cv_ref, _, o_ref, rows, kbuf, vbuf, sbuf, sems, row_sems
):
    width = o_ref.shape[1]
    q_ref, kn_ref, vn_ref = rows.at[0], rows.at[1], rows.at[2]
    early = fetch([(q_hbm, q_ref), (kn_hbm, kn_ref), (vn_hbm, vn_ref)], row_sems)
    scale = 1.0 / math.sqrt(DH)
    lanes = lax.broadcasted_iota(jnp.int32, (NEW, 2 * LANE), 1)
    rows = lax.broadcasted_iota(jnp.int32, (2 * NEW, NEW), 0)
    cols = lax.broadcasted_iota(jnp.int32, (2 * NEW, NEW), 1)
    causal = cols <= jnp.where(rows >= NEW, rows - NEW, rows)

    def run(length):
        step = min(KEYS, length)

        def copy(which, chunk):
            source, target = ((ck_ref, kbuf), (cv_ref, vbuf))[which]
            at = pl.ds(chunk * step, step)
            return pltpu.make_async_copy(
                source.at[0, at, :], target.at[at, :], sems.at[which, chunk]
            )

        for which in range(2):
            for chunk in range(length // step):
                copy(which, chunk).start()
        arrived = set()
        wait(early)

        def need(which, chunk):
            if (which, chunk) not in arrived:
                arrived.add((which, chunk))
                copy(which, chunk).wait()

        for group in range(width // GROUP):
            for half in range(2):
                tile = group * 3 + half
                window = pl.ds(tile * LANE, 2 * LANE)
                first_col = 64 * half
                in_a = (lanes >= first_col) & (lanes < first_col + DH)
                in_b = (lanes >= first_col + DH) & (lanes < first_col + 2 * DH)
                q_window = q_ref[:, window].astype(F32)
                pair = jnp.concatenate(
                    [jnp.where(in_a, q_window, 0.0), jnp.where(in_b, q_window, 0.0)], axis=0
                ).astype(BF16)

                def score(keys):
                    return (
                        lax.dot_general(
                            pair, keys, (((1,), (1,)), ((), ())), preferred_element_type=F32
                        )
                        * scale
                    )

                fresh = jnp.where(causal, score(kn_ref[:, window]), -1e30)
                top = fresh
                for start in range(0, length, step):
                    need(0, start // step)
                    scores = score(kbuf[pl.ds(start, step), window])
                    sbuf[:, pl.ds(start, step)] = scores
                    for lane in range(0, step, LANE):
                        top = jnp.maximum(top, scores[:, lane : lane + LANE])
                highest = jnp.max(top, axis=1, keepdims=True)
                weights = jnp.exp(fresh - highest)
                total = weights
                mixed = jnp.dot(
                    weights.astype(BF16), vn_ref[:, window], preferred_element_type=F32
                )
                for start in range(0, length, step):
                    need(1, start // step)
                    weights = jnp.exp(sbuf[:, pl.ds(start, step)] - highest)
                    for lane in range(0, step, LANE):
                        total = total + weights[:, lane : lane + LANE]
                    mixed = mixed + jnp.dot(
                        weights.astype(BF16),
                        vbuf[pl.ds(start, step), window],
                        preferred_element_type=F32,
                    )
                mixed = mixed / jnp.sum(total, axis=1, keepdims=True)
                before = o_ref[:, window].astype(F32) if half else 0.0
                o_ref[:, window] = jnp.where(
                    in_a, mixed[:NEW], jnp.where(in_b, mixed[NEW:], before)
                ).astype(BF16)

    long = len_ref[0] > SHORT

    @pl.when(long)
    def _():
        run(CACHE)

    @pl.when(jnp.logical_not(long))
    def _():
        run(SHORT)


def attend(queries, key_new, value_new, cache_keys, cache_values, cached_len, after):
    width = queries.shape[1]
    (attended,) = call(
        attention_kernel,
        [((NEW, width), BF16)],
        [
            (cached_len, pl.BlockSpec(memory_space=pltpu.SMEM)),
            *anywhere(queries, key_new, value_new, cache_keys, cache_values, after),
        ],
        [
            pltpu.VMEM((3, NEW, width), BF16),
            pltpu.VMEM((CACHE, width), BF16),
            pltpu.VMEM((CACHE, width), BF16),
            pltpu.VMEM((2 * NEW, CACHE), F32),
            pltpu.SemaphoreType.DMA((2, CACHE // KEYS)),
            pltpu.SemaphoreType.DMA((3,)),
        ],
        flops=8 * NEW * CACHE * width,
        limit=50,
    )
    return attended


def rotation_tables(cached_len):
    half = ROT // 2
    feature = np.arange(GROUP) % DH
    exponent = jnp.asarray((feature % half).astype(np.float32)) * (2.0 / ROT)
    frequency = jnp.power(10000.0, -exponent)
    position = cached_len.astype(F32) + jnp.arange(NEW, dtype=F32)
    angle = position[:, None] * frequency[None, :]
    lower, upper = jnp.asarray(feature < half), jnp.asarray((feature >= half) & (feature < ROT))
    cosine, sine = jnp.cos(angle), jnp.sin(angle)
    return (
        jnp.where(lower | upper, cosine, 1.0),
        jnp.where(lower, -sine, 0.0),
        jnp.where(upper, sine, 0.0),
    )


def cut_kernel(left_ref, right_ref, left, right):
    left[...] = left_ref[:, : left.shape[1]]
    right[...] = right_ref[:, left.shape[1] :]


def gather_weights_kernel(down_ref, out_ref, _, weights, semaphores):
    rows = down_ref.shape[0]
    wait(
        fetch(
            [
                (down_ref, weights.at[pl.ds(0, rows), :]),
                (out_ref, weights.at[pl.ds(rows, out_ref.shape[0]), :]),
            ],
            semaphores,
        )
    )


def out_kernel(layout, rows, masks, weights, *refs):
    inputs, outs, total = list(refs), refs[-1 - masks : -1], refs[-1]
    head = lax.axis_index("head")
    for i, pieces in enumerate(layout):
        term = None
        for begin in pieces:
            ref = inputs.pop(0)
            product = jnp.dot(
                ref[...], weights[pl.ds(begin, ref.shape[1]), :], preferred_element_type=F32
            )
            term = product if term is None else term + product
        total[...] = term
        for mask, out in enumerate(outs):
            at = pl.ds(pl.multiple_of((head ^ mask) * rows, rows), rows)
            out[i * rows : (i + 1) * rows, :] = total[at, :]


def final_kernel(count, indices, *refs):
    terms, (residual_ref, local_ref) = refs[:count], refs[count : count + 2]
    outs, (residual, local, semaphores) = refs[-3 - len(indices) : -3], refs[-3:]
    rows, part = outs[0].shape
    pairs = [(local_ref, local)]
    for i, index in enumerate(indices):
        pairs.append((residual_ref.at[pl.ds(index * rows, rows), :], residual.at[i]))
    wait(fetch(pairs, semaphores))
    for i, out in enumerate(outs):
        total = residual[i][:, :part].astype(F32)
        for term in terms:
            total = total + term[i * rows : (i + 1) * rows, :]
        out[...] = (total + local[4:5, :]).astype(BF16)


def assemble_kernel(order, batches, rows, masks, *refs):
    out, refs = refs[-1], list(refs[:-1])
    part = refs[0].shape[1]
    head = lax.axis_index("head")
    for batch in batches:
        for mask in range(masks):
            piece = refs.pop(0)
            at = pl.ds(pl.multiple_of((head ^ mask) * rows, rows), rows)
            for i, distance in enumerate(batch):
                first = pl.multiple_of(block_at(order, -distance) * part, LANE)
                out[at, pl.ds(first, part)] = piece[i * rows : (i + 1) * rows, :]


def body(
    req_size,
    head_size,
    hidden,
    attn_norm_gain,
    attn_norm_bias,
    mlp_norm_gain,
    mlp_norm_bias,
    qkv_weight,
    qkv_bias,
    out_weight,
    out_bias,
    up_weight,
    up_bias,
    down_weight,
    down_bias,
    cache_keys,
    cache_values,
    cached_len,
):
    order = ring_order(req_size)
    far = req_size // 2
    tokens, model = hidden.shape
    part = model // req_size
    rows = tokens // head_size
    bits = head_size.bit_length() - 1
    qkv_width, up_width = qkv_weight.shape[1], up_weight.shape[1]
    width = qkv_width // 3
    heads = qkv_width // (3 * GROUP)

    def shift(values, distance):
        pairs = [(order[i], order[(i + distance) % req_size]) for i in range(req_size)]
        return lax.ppermute(values, "req", pairs)

    def swap(values, mask):
        return lax.ppermute(values, "head", [(i, i ^ mask) for i in range(head_size)])

    def straight(values, distance, mask):
        pairs = [
            (order[i] * head_size + h, order[(i + distance) % req_size] * head_size + (h ^ mask))
            for i in range(req_size)
            for h in range(head_size)
        ]
        return lax.ppermute(values, ("req", "head"), pairs)

    def exchange(values):
        held = {0: values}
        for bit in reversed(range(bits)):
            for mask in sorted(held):
                held[mask | 1 << bit] = swap(held[mask], 1 << bit)
        return [held[mask] for mask in range(head_size)]

    distances = list(range(1 - far, far + 1))
    outer = [far, far - 1, 1 - far]
    inner = [d for d in distances if d not in outer]

    wanted = outer + inner
    sent = call(
        functools.partial(message_kernel, order, wanted),
        [((rows, part + LANE), BF16)] * len(wanted),
        anywhere(hidden),
        [pltpu.VMEM((rows, model), BF16), pltpu.SemaphoreType.DMA],
        limit=56,
    )
    got = [shift(m, -d) if d else m for m, d in zip(sent, wanted)]

    def stacked(blocks, after=()):
        (result,) = call(
            functools.partial(stack_kernel, len(blocks)),
            [((len(blocks) * blocks[0].shape[0], blocks[0].shape[1]), BF16)],
            [*blocks, *anywhere(*after)],
        )
        return result

    vectors = [
        v.reshape(-1, LANE)
        for v in (attn_norm_gain, attn_norm_bias, mlp_norm_gain, mlp_norm_bias, out_bias, down_bias)
    ]
    tables = rotation_tables(cached_len)
    (heads_weight,) = call(
        prepare_kernel,
        [((part, qkv_width), BF16)],
        [qkv_weight, *anywhere(sent[0])],
        flops=2 * part * qkv_width * GROUP,
    )
    outer_stack = stacked(got[: len(outer)], [heads_weight, *got[len(outer) :]])
    heads_bias, local = call(
        local_kernel,
        [((1, qkv_width), F32), ((8, part), F32)],
        [qkv_bias.reshape(-1, LANE), *vectors, *anywhere(outer_stack)],
    )
    inner_stack = stacked(got[len(outer) :])
    groups = [exchange(outer_stack), exchange(inner_stack)]
    places = {d: (g, i) for g, group in enumerate((outer, inner)) for i, d in enumerate(group)}

    def pieces_of(d):
        return anywhere(*groups[places[d][0]])

    def buffers(count, *more):
        return [
            pltpu.VMEM((count, NEW, part + LANE), BF16),
            pltpu.VMEM((8, part), F32),
            *more,
            pltpu.SemaphoreType.DMA((count * head_size + 5,)),
        ]

    kinds = [
        (qkv_chunks, qkv_emit, 0, heads_weight, 4 * GROUP * heads),
        (up_chunks, up_emit, 2, up_weight, up_width),
    ]
    moving = [None, None]
    after = inner_stack
    for left in range(far, 0, -1):
        for kind, (chunks, emit, first, weight, out_width) in enumerate(kinds):
            if left == far:
                results = call(
                    functools.partial(far_kernel, chunks, emit, first, places[far][1], head_size),
                    [((NEW, out_width // 2), BF16)] * 2,
                    [*pieces_of(far), *anywhere(local), weight, *anywhere(after)],
                    buffers(1),
                    flops=2 * NEW * weight.size,
                )
            else:
                indices = [places[left][1], places[-left][1]]
                results = call(
                    functools.partial(step_kernel, chunks, emit, first, indices, head_size),
                    [((NEW, out_width), BF16)] * 2,
                    [
                        *pieces_of(left),
                        *pieces_of(-left),
                        *anywhere(local),
                        weight,
                        *moving[kind],
                        *anywhere(after),
                    ],
                    buffers(2),
                    flops=4 * NEW * weight.size,
                )
            after = results[0]
            moving[kind] = [shift(results[0], 1), shift(results[1], -1)]

    index = places[0][1]
    queries, key_rows, value_rows = call(
        functools.partial(heads_kernel, index, head_size),
        [((NEW, width), BF16)] * 3,
        [
            *pieces_of(0),
            *anywhere(local),
            heads_weight,
            *anywhere(heads_bias, *tables),
            *moving[0],
            *anywhere(after),
        ],
        buffers(1, pltpu.VMEM((1, qkv_width), F32), pltpu.VMEM((3, NEW, GROUP), F32)),
        flops=2 * NEW * heads_weight.size,
    )
    attended = attend(
        queries, key_rows, value_rows, cache_keys, cache_values, cached_len, after
    )
    bias_rows = up_bias.reshape(-1, LANE)
    full_width = up_width + width
    (block,) = call(
        functools.partial(units_kernel, index, head_size),
        [((NEW, full_width), BF16)],
        [
            *pieces_of(0),
            *anywhere(local),
            up_weight,
            *anywhere(bias_rows),
            *moving[1],
            attended,
        ],
        buffers(1, pltpu.VMEM(bias_rows.shape, F32)),
        flops=2 * NEW * up_weight.size,
    )

    blocks = {0: block}
    for step in range(1, far):
        for sign in (1, -1):
            blocks[-sign * step] = shift(blocks[-sign * (step - 1)], sign)
    cut = full_width // (2 * LANE) * LANE
    halves = call(
        cut_kernel,
        [((NEW, cut), BF16), ((NEW, full_width - cut), BF16)],
        [blocks[1 - far], blocks[far - 1]],
    )
    far_halves = [shift(halves[0], 1), shift(halves[1], -1)]

    (out_weights,) = call(
        gather_weights_kernel,
        [((full_width, part), BF16)],
        anywhere(down_weight, out_weight, block),
        [pltpu.SemaphoreType.DMA((2,))],
    )

    def products(batch, after):
        layout = [[0, cut] if d == far else [0] for d in batch]
        args = [a for d in batch for a in (far_halves if d == far else [blocks[d]])]
        return call(
            functools.partial(out_kernel, layout, rows, head_size),
            [((len(batch) * rows, part), F32)] * head_size,
            [out_weights, *args, *anywhere(*after)],
            [pltpu.VMEM((NEW, part), F32)],
            flops=2 * len(batch) * NEW * out_weights.size,
        )

    def finish(batch, terms, after):
        indices = [places[d][1] for d in batch]
        (group,) = {places[d][0] for d in batch}
        residual = groups[group][0]
        return call(
            functools.partial(final_kernel, len(terms), indices),
            [((rows, part), BF16)] * len(batch),
            [*terms, *anywhere(residual, local, *after)],
            [
                pltpu.VMEM((len(batch), rows, part + LANE), BF16),
                pltpu.VMEM((8, part), F32),
                pltpu.SemaphoreType.DMA((len(batch) + 1,)),
            ],
        )

    def halved(terms):
        held = dict(enumerate(terms))
        for bit in range(bits):
            leaving = [m for m in held if m >> bit & 1]
            arrived = {m: swap(held[m], 1 << bit) for m in leaving}
            if bit < bits - 1:
                for m in leaving:
                    held[m ^ 1 << bit] = held[m ^ 1 << bit] + arrived[m]
                    del held[m]
        return [held[0], arrived[1 << bits - 1]]

    def homeward(ready, batch):
        return [shift(b, d) if d else b for b, d in zip(ready, batch)]

    batches = [[0, 1, -1], *([d, -d] for d in range(2, far)), [far]]
    homes, after = [], []
    for batch in batches[:-2]:
        ready = finish(batch, halved(products(batch, after)), [])
        homes.append(homeward(ready, batch))
        after = [ready[0]]
    near, last = batches[-2:]
    near_terms = halved(products(near, [*after, halves[0]]))
    terms = products(last, [])
    homes.append(homeward(finish(near, near_terms, [terms[0]]), near))
    pieces = [piece for home in homes for piece in exchange(stacked(home))]
    (block,) = finish(last, [terms[0]] + [swap(terms[m], m) for m in range(1, head_size)], [])
    pieces += [straight(block, far, mask) for mask in range(head_size)]
    (result,) = call(
        functools.partial(assemble_kernel, order, batches, rows, head_size),
        [((tokens, model), BF16)],
        pieces,
    )
    return result, key_rows[None], value_rows[None]


def solution(mesh):
    return jax.shard_map(
        functools.partial(body, mesh.shape["req"], mesh.shape["head"]),
        mesh=mesh,
        in_specs=(
            P("req", None),
            P(),
            P(),
            P(),
            P(),
            P("req", "head"),
            P("head"),
            P("head", "req"),
            P(),
            P("req", "head"),
            P("head"),
            P("head", "req"),
            P(),
            P("req", None, "head"),
            P("req", None, "head"),
            P("req"),
        ),
        out_specs=(P("req", None), P("req", None, "head"), P("req", None, "head")),
        check_vma=False,
    )
```

```python
import functools
import math

import jax
import jax.numpy as jnp
import numpy as np
from jax import lax
from jax.experimental import pallas as pl
from jax.experimental.pallas import tpu as pltpu
from jax.sharding import PartitionSpec as P

DH = 96
ROT = 24
NEW = 128
CACHE = 4096
SHORT = 128
GROUP = 4 * DH
LANE = 128
KEYS = 1024
CHUNK = 384
F32 = jnp.float32
BF16 = jnp.bfloat16
MIB = 1024 * 1024


def ring_order(size):
    inner = 1
    while 4 * inner * inner <= size:
        inner *= 2
    outer = size // inner
    order = [a * inner for a in range(outer)]
    forward = True
    for a in reversed(range(outer)):
        row = list(range(1, inner))
        order += [a * inner + b for b in (row if forward else row[::-1])]
        forward = not forward
    return order


def pick(table, index):
    value = jnp.int32(table[0])
    for i in range(1, len(table)):
        value = jnp.where(index == i, jnp.int32(table[i]), value)
    return value


def block_at(order, distance):
    size = len(order)
    here = lax.axis_index("req")
    return pick([order[(order.index(i) + distance) % size] for i in range(size)], here)


ANYWHERE = pl.BlockSpec(memory_space=pl.ANY)
ON_CHIP = pl.BlockSpec(memory_space=pltpu.VMEM)


def call(kernel, outs, args, scratch=(), flops=0, limit=32):
    args = [a if isinstance(a, tuple) else (a, ON_CHIP) for a in args]
    return pl.pallas_call(
        kernel,
        out_shape=[jax.ShapeDtypeStruct(*o) for o in outs],
        in_specs=[spec for _, spec in args],
        out_specs=[ON_CHIP] * len(outs),
        scratch_shapes=list(scratch),
        compiler_params=pltpu.CompilerParams(vmem_limit_bytes=limit * MIB),
        cost_estimate=pl.CostEstimate(
            flops=flops,
            bytes_accessed=sum(math.prod(shape) * 4 for shape, _ in outs),
            transcendentals=0,
        ),
    )(*(a for a, _ in args))


def anywhere(*arrays):
    return [(a, ANYWHERE) for a in arrays]


def fetch(pairs, semaphores, first=0):
    copies = [
        pltpu.make_async_copy(source, target, semaphores.at[first + i])
        for i, (source, target) in enumerate(pairs)
    ]
    for copy in copies:
        copy.start()
    return copies


def wait(copies):
    for copy in copies:
        copy.wait()


def rows_pairs(pieces, index, raw):
    head = lax.axis_index("head")
    rows = raw.shape[0] // len(pieces)
    return [
        (
            piece.at[pl.ds(index * rows, rows), :],
            raw.at[pl.ds(pl.multiple_of((head ^ mask) * rows, rows), rows), :],
        )
        for mask, piece in enumerate(pieces)
    ]


def wide(ref, first, count):
    return jnp.concatenate([ref[i : i + 1, :] for i in range(first, first + count)], axis=1)


def split_float(values, count):
    pieces = []
    for _ in range(count):
        piece = values.astype(BF16)
        pieces.append(piece)
        values = values - piece.astype(F32)
    return pieces


def message_kernel(order, distances, hidden_ref, *refs):
    outs, (buffer, semaphore) = refs[-2 - len(distances) : -2], refs[-2:]
    rows, width = outs[0].shape
    part = width - LANE
    mine = pl.ds(pl.multiple_of(lax.axis_index("head") * rows, rows), rows)
    copy = pltpu.make_async_copy(hidden_ref.at[mine, :], buffer, semaphore)
    copy.start()
    copy.wait()
    widened = buffer[...].astype(F32)
    center = jnp.mean(widened, axis=-1, keepdims=True)
    spread = jnp.mean(jnp.square(widened - center), axis=-1, keepdims=True)
    pieces = split_float(center, 3) + split_float(lax.rsqrt(spread + 1e-05), 3)
    lanes = lax.broadcasted_iota(jnp.int32, (rows, LANE), 1)
    stats = jnp.zeros((rows, LANE), F32)
    for i, piece in enumerate(pieces):
        stats = jnp.where(lanes == i, piece.astype(F32), stats)
    stats = stats.astype(BF16)
    for out, distance in zip(outs, distances):
        first = pl.multiple_of(block_at(order, -distance) * part, LANE)
        out[:, :part] = buffer[:, pl.ds(first, part)]
        out[:, part:] = stats


def stack_kernel(count, *refs):
    out = refs[-1]
    rows = out.shape[0] // count
    for i in range(count):
        out[i * rows : (i + 1) * rows, :] = refs[i][...]


def reordered(values):
    return jnp.concatenate(
        [
            values[:, (3 * h + kind) * DH : (3 * h + kind + 1) * DH]
            for kind in range(3)
            for h in range(GROUP // DH)
        ],
        axis=1,
    )


def prepare_kernel(weight_ref, *refs):
    out = refs[-1]
    span = 3 * GROUP
    for c in range(weight_ref.shape[1] // span):
        at = pl.ds(c * span, span)

        def strip(r, _, at=at):
            rows = pl.ds(pl.multiple_of(r * 64, 64), 64)
            out[rows, at] = reordered(weight_ref[rows, at])
            return 0

        lax.fori_loop(0, weight_ref.shape[0] // 64, strip, 0)


def local_kernel(bias, *refs):
    vectors, (bias_out, local_ref) = refs[:6], refs[-2:]
    span = 3 * GROUP
    for c in range(bias_out.shape[1] // span):
        row = wide(bias, c * span // LANE, span // LANE)
        bias_out[:, pl.ds(c * span, span)] = reordered(jnp.broadcast_to(row, (8, span)))[0:1]
    part = local_ref.shape[1]
    first = lax.axis_index("req") * (part // LANE)
    for i in range(part // LANE):
        at = pl.ds(i * LANE, LANE)
        rows_of = [v[pl.ds(first + i, 1), :] for v in vectors]
        for j in range(4):
            local_ref[j : j + 1, at] = rows_of[j]
        local_ref[4:5, at] = rows_of[4] + rows_of[5]
        local_ref[5:8, at] = jnp.zeros((3, LANE), F32)


def normed(raw, local_ref, first):
    part = raw.shape[1] - LANE
    stats = raw[:, part:].astype(F32)
    center = stats[:, 0:1] + stats[:, 1:2] + stats[:, 2:3]
    scale = stats[:, 3:4] + stats[:, 4:5] + stats[:, 5:6]
    normal = (raw[:, :part].astype(F32) - center) * scale
    return (
        normal * local_ref[first : first + 1, :] + local_ref[first + 1 : first + 2, :]
    ).astype(BF16)


def up_chunks(width):
    return [(pl.ds(c, CHUNK), pl.ds(c, CHUNK)) for c in range(0, width, CHUNK)]


def up_emit(values, old, _):
    if old is not None:
        values = values + old.astype(F32)
    return values.astype(BF16)


def qkv_chunks(width):
    chunks = []
    for c in range(width // (3 * GROUP)):
        source, target = 3 * c * GROUP, 4 * c * GROUP
        chunks.append((pl.ds(source, GROUP), pl.ds(target, 2 * GROUP)))
        chunks.append((pl.ds(source + GROUP, 2 * GROUP), pl.ds(target + 2 * GROUP, 2 * GROUP)))
    return chunks


def qkv_emit(values, old, source):
    if source.size == 2 * GROUP:
        return up_emit(values, old, source)
    if old is not None:
        values = values + old[:, :GROUP].astype(F32) + old[:, GROUP:].astype(F32)
    return jnp.concatenate(split_float(values, 2), axis=1)


def far_kernel(chunks, emit, first, index, masks, *refs):
    pieces, (local_ref, weight_ref, _) = refs[:masks], refs[masks : masks + 3]
    forward, backward, raw, local, semaphores = refs[masks + 3 :]
    wait(fetch([(local_ref, local)] + rows_pairs(pieces, index, raw.at[0]), semaphores))
    block = normed(raw.at[0], local, first)
    half = forward.shape[1]
    for source, target in chunks(weight_ref.shape[1]):
        product = jnp.dot(block, weight_ref[:, source], preferred_element_type=F32)
        out, begin = (forward, 0) if target.start < half else (backward, half)
        out[:, pl.ds(target.start - begin, target.size)] = emit(product, None, source)


def step_kernel(chunks, emit, first, indices, masks, *refs):
    pieces = [refs[b * masks : (b + 1) * masks] for b in range(2)]
    local_ref, weight_ref, *received, _ = refs[2 * masks : 2 * masks + 5]
    *outs, raw, local, semaphores = refs[2 * masks + 5 :]
    pairs = [(local_ref, local)]
    for b, index in enumerate(indices):
        pairs += rows_pairs(pieces[b], index, raw.at[b])
    wait(fetch(pairs, semaphores))
    stacked = jnp.concatenate([normed(raw.at[b], local, first) for b in range(2)], axis=0)
    for source, target in chunks(weight_ref.shape[1]):
        product = jnp.dot(stacked, weight_ref[:, source], preferred_element_type=F32)
        for i, (out, old) in enumerate(zip(outs, received)):
            width = old.shape[1]
            begin = i * (out.shape[1] - width)
            here = begin <= target.start < begin + width
            out[:, target] = emit(
                product[i * NEW : (i + 1) * NEW],
                old[:, pl.ds(target.start - begin, target.size)] if here else None,
                source,
            )


def units_kernel(index, masks, *refs):
    pieces = refs[:masks]
    local_ref, weight_ref, bias_ref, plus, minus, attended, out = refs[masks : masks + 7]
    raw, local, bias, semaphores = refs[masks + 7 :]
    pairs = [(local_ref, local), (bias_ref, bias)] + rows_pairs(pieces, index, raw.at[0])
    wait(fetch(pairs, semaphores))
    block = normed(raw.at[0], local, 2)
    width = weight_ref.shape[1]
    for at, _ in up_chunks(width):
        total = jnp.dot(block, weight_ref[:, at], preferred_element_type=F32)
        total = total + wide(bias, at.start // LANE, CHUNK // LANE)
        total = total + plus[:, at].astype(F32) + minus[:, at].astype(F32)
        out[:, at] = jax.nn.gelu(total, approximate=True).astype(BF16)
    out[:, width:] = attended[...]


def heads_kernel(index, masks, *refs):
    pieces = refs[:masks]
    local_ref, weight_ref, bias_ref, *table_refs = refs[masks : masks + 6]
    plus, minus, _, q_out, k_out, v_out, raw, local, bias, tables, semaphores = refs[masks + 6 :]
    pairs = [(local_ref, local), (bias_ref, bias)] + rows_pairs(pieces, index, raw.at[0])
    pairs += [(ref, tables.at[i]) for i, ref in enumerate(table_refs)]
    wait(fetch(pairs, semaphores))
    block = normed(raw.at[0], local, 0)
    half = ROT // 2
    cosine, from_above, from_below = tables[0], tables[1], tables[2]

    def rotate(values):
        above = pltpu.roll(values, GROUP - half, 1)
        below = pltpu.roll(values, half, 1)
        return (values * cosine + above * from_above + below * from_below).astype(BF16)

    for c in range(weight_ref.shape[1] // (3 * GROUP)):
        source = pl.ds(3 * c * GROUP, 3 * GROUP)
        total = jnp.dot(block, weight_ref[:, source], preferred_element_type=F32)
        total = total + bias[:, source]
        query, key, value = (total[:, i * GROUP : (i + 1) * GROUP] for i in range(3))
        for other in (plus, minus):
            high, low, other_key, other_value = (
                other[:, (4 * c + i) * GROUP : (4 * c + i + 1) * GROUP].astype(F32)
                for i in range(4)
            )
            query, key, value = query + high + low, key + other_key, value + other_value
        at = pl.ds(c * GROUP, GROUP)
        q_out[:, at] = rotate(query)
        k_out[:, at] = rotate(key)
        v_out[:, at] = value.astype(BF16)


def attention_kernel(
    len_ref, q_hbm, kn_hbm, vn_hbm, ck_ref, cv_ref, _, o_ref, rows, kbuf, vbuf, sbuf, sems, row_sems
):
    width = o_ref.shape[1]
    q_ref, kn_ref, vn_ref = rows.at[0], rows.at[1], rows.at[2]
    early = fetch([(q_hbm, q_ref), (kn_hbm, kn_ref), (vn_hbm, vn_ref)], row_sems)
    scale = 1.0 / math.sqrt(DH)
    lanes = lax.broadcasted_iota(jnp.int32, (NEW, 2 * LANE), 1)
    rows = lax.broadcasted_iota(jnp.int32, (2 * NEW, NEW), 0)
    cols = lax.broadcasted_iota(jnp.int32, (2 * NEW, NEW), 1)
    causal = cols <= jnp.where(rows >= NEW, rows - NEW, rows)

    def run(length):
        step = min(KEYS, length)

        def copy(which, chunk):
            source, target = ((ck_ref, kbuf), (cv_ref, vbuf))[which]
            at = pl.ds(chunk * step, step)
            return pltpu.make_async_copy(
                source.at[0, at, :], target.at[at, :], sems.at[which, chunk]
            )

        for which in range(2):
            for chunk in range(length // step):
                copy(which, chunk).start()
        arrived = set()
        wait(early)

        def need(which, chunk):
            if (which, chunk) not in arrived:
                arrived.add((which, chunk))
                copy(which, chunk).wait()

        for group in range(width // GROUP):
            for half in range(2):
                tile = group * 3 + half
                window = pl.ds(tile * LANE, 2 * LANE)
                first_col = 64 * half
                in_a = (lanes >= first_col) & (lanes < first_col + DH)
                in_b = (lanes >= first_col + DH) & (lanes < first_col + 2 * DH)
                q_window = q_ref[:, window].astype(F32)
                pair = jnp.concatenate(
                    [jnp.where(in_a, q_window, 0.0), jnp.where(in_b, q_window, 0.0)], axis=0
                ).astype(BF16)

                def score(keys):
                    return (
                        lax.dot_general(
                            pair, keys, (((1,), (1,)), ((), ())), preferred_element_type=F32
                        )
                        * scale
                    )

                fresh = jnp.where(causal, score(kn_ref[:, window]), -1e30)
                top = fresh
                for start in range(0, length, step):
                    need(0, start // step)
                    scores = score(kbuf[pl.ds(start, step), window])
                    sbuf[:, pl.ds(start, step)] = scores
                    for lane in range(0, step, LANE):
                        top = jnp.maximum(top, scores[:, lane : lane + LANE])
                highest = jnp.max(top, axis=1, keepdims=True)
                weights = jnp.exp(fresh - highest)
                total = weights
                mixed = jnp.dot(
                    weights.astype(BF16), vn_ref[:, window], preferred_element_type=F32
                )
                for start in range(0, length, step):
                    need(1, start // step)
                    weights = jnp.exp(sbuf[:, pl.ds(start, step)] - highest)
                    for lane in range(0, step, LANE):
                        total = total + weights[:, lane : lane + LANE]
                    mixed = mixed + jnp.dot(
                        weights.astype(BF16),
                        vbuf[pl.ds(start, step), window],
                        preferred_element_type=F32,
                    )
                mixed = mixed / jnp.sum(total, axis=1, keepdims=True)
                before = o_ref[:, window].astype(F32) if half else 0.0
                o_ref[:, window] = jnp.where(
                    in_a, mixed[:NEW], jnp.where(in_b, mixed[NEW:], before)
                ).astype(BF16)

    long = len_ref[0] > SHORT

    @pl.when(long)
    def _():
        run(CACHE)

    @pl.when(jnp.logical_not(long))
    def _():
        run(SHORT)


def attend(queries, key_new, value_new, cache_keys, cache_values, cached_len, after):
    width = queries.shape[1]
    (attended,) = call(
        attention_kernel,
        [((NEW, width), BF16)],
        [
            (cached_len, pl.BlockSpec(memory_space=pltpu.SMEM)),
            *anywhere(queries, key_new, value_new, cache_keys, cache_values, after),
        ],
        [
            pltpu.VMEM((3, NEW, width), BF16),
            pltpu.VMEM((CACHE, width), BF16),
            pltpu.VMEM((CACHE, width), BF16),
            pltpu.VMEM((2 * NEW, CACHE), F32),
            pltpu.SemaphoreType.DMA((2, CACHE // KEYS)),
            pltpu.SemaphoreType.DMA((3,)),
        ],
        flops=8 * NEW * CACHE * width,
        limit=50,
    )
    return attended


def rotation_tables(cached_len):
    half = ROT // 2
    feature = np.arange(GROUP) % DH
    exponent = jnp.asarray((feature % half).astype(np.float32)) * (2.0 / ROT)
    frequency = jnp.power(10000.0, -exponent)
    position = cached_len.astype(F32) + jnp.arange(NEW, dtype=F32)
    angle = position[:, None] * frequency[None, :]
    lower, upper = jnp.asarray(feature < half), jnp.asarray((feature >= half) & (feature < ROT))
    cosine, sine = jnp.cos(angle), jnp.sin(angle)
    return (
        jnp.where(lower | upper, cosine, 1.0),
        jnp.where(lower, -sine, 0.0),
        jnp.where(upper, sine, 0.0),
    )


def cut_kernel(left_ref, right_ref, left, right):
    left[...] = left_ref[:, : left.shape[1]]
    right[...] = right_ref[:, left.shape[1] :]


def gather_weights_kernel(down_ref, out_ref, _, weights, semaphores):
    rows = down_ref.shape[0]
    wait(
        fetch(
            [
                (down_ref, weights.at[pl.ds(0, rows), :]),
                (out_ref, weights.at[pl.ds(rows, out_ref.shape[0]), :]),
            ],
            semaphores,
        )
    )


def out_kernel(layout, rows, masks, weights, *refs):
    inputs, outs, total = list(refs), refs[-1 - masks : -1], refs[-1]
    head = lax.axis_index("head")
    for i, pieces in enumerate(layout):
        term = None
        for begin in pieces:
            ref = inputs.pop(0)
            product = jnp.dot(
                ref[...], weights[pl.ds(begin, ref.shape[1]), :], preferred_element_type=F32
            )
            term = product if term is None else term + product
        total[...] = term
        for mask, out in enumerate(outs):
            at = pl.ds(pl.multiple_of((head ^ mask) * rows, rows), rows)
            out[i * rows : (i + 1) * rows, :] = total[at, :]


def final_kernel(count, indices, *refs):
    terms, (residual_ref, local_ref) = refs[:count], refs[count : count + 2]
    outs, (residual, local, semaphores) = refs[-3 - len(indices) : -3], refs[-3:]
    rows, part = outs[0].shape
    pairs = [(local_ref, local)]
    for i, index in enumerate(indices):
        pairs.append((residual_ref.at[pl.ds(index * rows, rows), :], residual.at[i]))
    wait(fetch(pairs, semaphores))
    for i, out in enumerate(outs):
        total = residual[i][:, :part].astype(F32)
        for term in terms:
            total = total + term[i * rows : (i + 1) * rows, :]
        out[...] = (total + local[4:5, :]).astype(BF16)


def assemble_kernel(order, batches, rows, masks, *refs):
    out, refs = refs[-1], list(refs[:-1])
    part = refs[0].shape[1]
    head = lax.axis_index("head")
    for batch in batches:
        for mask in range(masks):
            piece = refs.pop(0)
            at = pl.ds(pl.multiple_of((head ^ mask) * rows, rows), rows)
            for i, distance in enumerate(batch):
                first = pl.multiple_of(block_at(order, -distance) * part, LANE)
                out[at, pl.ds(first, part)] = piece[i * rows : (i + 1) * rows, :]


def body(
    req_size,
    head_size,
    hidden,
    attn_norm_gain,
    attn_norm_bias,
    mlp_norm_gain,
    mlp_norm_bias,
    qkv_weight,
    qkv_bias,
    out_weight,
    out_bias,
    up_weight,
    up_bias,
    down_weight,
    down_bias,
    cache_keys,
    cache_values,
    cached_len,
):
    order = ring_order(req_size)
    far = req_size // 2
    tokens, model = hidden.shape
    part = model // req_size
    rows = tokens // head_size
    bits = head_size.bit_length() - 1
    qkv_width, up_width = qkv_weight.shape[1], up_weight.shape[1]
    width = qkv_width // 3
    heads = qkv_width // (3 * GROUP)

    def shift(values, distance):
        pairs = [(order[i], order[(i + distance) % req_size]) for i in range(req_size)]
        return lax.ppermute(values, "req", pairs)

    def swap(values, mask):
        return lax.ppermute(values, "head", [(i, i ^ mask) for i in range(head_size)])

    def straight(values, distance, mask):
        pairs = [
            (order[i] * head_size + h, order[(i + distance) % req_size] * head_size + (h ^ mask))
            for i in range(req_size)
            for h in range(head_size)
        ]
        return lax.ppermute(values, ("req", "head"), pairs)

    def exchange(values):
        held = {0: values}
        for bit in reversed(range(bits)):
            for mask in sorted(held):
                held[mask | 1 << bit] = swap(held[mask], 1 << bit)
        return [held[mask] for mask in range(head_size)]

    distances = list(range(1 - far, far + 1))
    outer = [far, far - 1, 1 - far]
    inner = [d for d in distances if d not in outer]

    wanted = outer + inner
    sent = call(
        functools.partial(message_kernel, order, wanted),
        [((rows, part + LANE), BF16)] * len(wanted),
        anywhere(hidden),
        [pltpu.VMEM((rows, model), BF16), pltpu.SemaphoreType.DMA],
        limit=56,
    )
    got = [shift(m, -d) if d else m for m, d in zip(sent, wanted)]

    def stacked(blocks, after=()):
        (result,) = call(
            functools.partial(stack_kernel, len(blocks)),
            [((len(blocks) * blocks[0].shape[0], blocks[0].shape[1]), BF16)],
            [*blocks, *anywhere(*after)],
        )
        return result

    vectors = [
        v.reshape(-1, LANE)
        for v in (attn_norm_gain, attn_norm_bias, mlp_norm_gain, mlp_norm_bias, out_bias, down_bias)
    ]
    tables = rotation_tables(cached_len)
    (heads_weight,) = call(
        prepare_kernel,
        [((part, qkv_width), BF16)],
        [qkv_weight, *anywhere(sent[0])],
        flops=2 * part * qkv_width * GROUP,
    )
    outer_stack = stacked(got[: len(outer)], [heads_weight, *got[len(outer) :]])
    heads_bias, local = call(
        local_kernel,
        [((1, qkv_width), F32), ((8, part), F32)],
        [qkv_bias.reshape(-1, LANE), *vectors, *anywhere(outer_stack)],
    )
    inner_stack = stacked(got[len(outer) :])
    groups = [exchange(outer_stack), exchange(inner_stack)]
    places = {d: (g, i) for g, group in enumerate((outer, inner)) for i, d in enumerate(group)}

    def pieces_of(d):
        return anywhere(*groups[places[d][0]])

    def buffers(count, *more):
        return [
            pltpu.VMEM((count, NEW, part + LANE), BF16),
            pltpu.VMEM((8, part), F32),
            *more,
            pltpu.SemaphoreType.DMA((count * head_size + 5,)),
        ]

    kinds = [
        (qkv_chunks, qkv_emit, 0, heads_weight, 4 * GROUP * heads),
        (up_chunks, up_emit, 2, up_weight, up_width),
    ]
    moving = [None, None]
    after = inner_stack
    for left in range(far, 0, -1):
        for kind, (chunks, emit, first, weight, out_width) in enumerate(kinds):
            if left == far:
                results = call(
                    functools.partial(far_kernel, chunks, emit, first, places[far][1], head_size),
                    [((NEW, out_width // 2), BF16)] * 2,
                    [*pieces_of(far), *anywhere(local), weight, *anywhere(after)],
                    buffers(1),
                    flops=2 * NEW * weight.size,
                )
            else:
                indices = [places[left][1], places[-left][1]]
                results = call(
                    functools.partial(step_kernel, chunks, emit, first, indices, head_size),
                    [((NEW, out_width), BF16)] * 2,
                    [
                        *pieces_of(left),
                        *pieces_of(-left),
                        *anywhere(local),
                        weight,
                        *moving[kind],
                        *anywhere(after),
                    ],
                    buffers(2),
                    flops=4 * NEW * weight.size,
                )
            after = results[0]
            moving[kind] = [shift(results[0], 1), shift(results[1], -1)]

    index = places[0][1]
    queries, key_rows, value_rows = call(
        functools.partial(heads_kernel, index, head_size),
        [((NEW, width), BF16)] * 3,
        [
            *pieces_of(0),
            *anywhere(local),
            heads_weight,
            *anywhere(heads_bias, *tables),
            *moving[0],
            *anywhere(after),
        ],
        buffers(1, pltpu.VMEM((1, qkv_width), F32), pltpu.VMEM((3, NEW, GROUP), F32)),
        flops=2 * NEW * heads_weight.size,
    )
    attended = attend(
        queries, key_rows, value_rows, cache_keys, cache_values, cached_len, after
    )
    bias_rows = up_bias.reshape(-1, LANE)
    full_width = up_width + width
    (block,) = call(
        functools.partial(units_kernel, index, head_size),
        [((NEW, full_width), BF16)],
        [
            *pieces_of(0),
            *anywhere(local),
            up_weight,
            *anywhere(bias_rows),
            *moving[1],
            attended,
        ],
        buffers(1, pltpu.VMEM(bias_rows.shape, F32)),
        flops=2 * NEW * up_weight.size,
    )

    blocks = {0: block}
    for step in range(1, far):
        for sign in (1, -1):
            blocks[-sign * step] = shift(blocks[-sign * (step - 1)], sign)
    cut = full_width // (2 * LANE) * LANE
    halves = call(
        cut_kernel,
        [((NEW, cut), BF16), ((NEW, full_width - cut), BF16)],
        [blocks[1 - far], blocks[far - 1]],
    )
    far_halves = [shift(halves[0], 1), shift(halves[1], -1)]

    (out_weights,) = call(
        gather_weights_kernel,
        [((full_width, part), BF16)],
        anywhere(down_weight, out_weight, block),
        [pltpu.SemaphoreType.DMA((2,))],
    )

    def products(batch, after):
        layout = [[0, cut] if d == far else [0] for d in batch]
        args = [a for d in batch for a in (far_halves if d == far else [blocks[d]])]
        return call(
            functools.partial(out_kernel, layout, rows, head_size),
            [((len(batch) * rows, part), F32)] * head_size,
            [out_weights, *args, *anywhere(*after)],
            [pltpu.VMEM((NEW, part), F32)],
            flops=2 * len(batch) * NEW * out_weights.size,
        )

    def finish(batch, terms, after):
        indices = [places[d][1] for d in batch]
        (group,) = {places[d][0] for d in batch}
        residual = groups[group][0]
        return call(
            functools.partial(final_kernel, len(terms), indices),
            [((rows, part), BF16)] * len(batch),
            [*terms, *anywhere(residual, local, *after)],
            [
                pltpu.VMEM((len(batch), rows, part + LANE), BF16),
                pltpu.VMEM((8, part), F32),
                pltpu.SemaphoreType.DMA((len(batch) + 1,)),
            ],
        )

    def halved(terms):
        held = dict(enumerate(terms))
        for bit in range(bits):
            leaving = [m for m in held if m >> bit & 1]
            arrived = {m: swap(held[m], 1 << bit) for m in leaving}
            if bit < bits - 1:
                for m in leaving:
                    held[m ^ 1 << bit] = held[m ^ 1 << bit] + arrived[m]
                    del held[m]
        return [held[0], arrived[1 << bits - 1]]

    def homeward(ready, batch):
        return [shift(b, d) if d else b for b, d in zip(ready, batch)]

    batches = [[0, 1, -1], *([d, -d] for d in range(2, far)), [far]]
    homes, after = [], []
    for batch in batches[:-2]:
        ready = finish(batch, halved(products(batch, after)), [])
        homes.append(homeward(ready, batch))
        after = [ready[0]]
    near, last = batches[-2:]
    near_terms = halved(products(near, [*after, halves[0]]))
    terms = products(last, [])
    homes.append(homeward(finish(near, near_terms, [terms[0]]), near))
    pieces = [piece for home in homes for piece in exchange(stacked(home))]
    (block,) = finish(last, [terms[0]] + [swap(terms[m], m) for m in range(1, head_size)], [])
    pieces += [straight(block, far, mask) for mask in range(head_size)]
    (result,) = call(
        functools.partial(assemble_kernel, order, batches, rows, head_size),
        [((tokens, model), BF16)],
        pieces,
    )
    return result, key_rows[None], value_rows[None]


def solution(mesh):
    return jax.shard_map(
        functools.partial(body, mesh.shape["req"], mesh.shape["head"]),
        mesh=mesh,
        in_specs=(
            P("req", None),
            P(),
            P(),
            P(),
            P(),
            P("req", "head"),
            P("head"),
            P("head", "req"),
            P(),
            P("req", "head"),
            P("head"),
            P("head", "req"),
            P(),
            P("req", None, "head"),
            P("req", None, "head"),
            P("req"),
        ),
        out_specs=(P("req", None), P("req", None, "head"), P("req", None, "head")),
        check_vma=False,
    )
```
